128 devices in a mesh: zc: 16 (over y, z), zl: 8 (over x, core).
Axes of the slice: x: 4, y: 4, z: 4, core: 2. Of those that a mesh axis runs over, the one named last changes fastest.
Arguments:
- velocity: float32 [8192, 3, 1536], P(('zc', 'zl')), may hold values from -6 to 6
- base_flow: float32 [192], replicated, may hold values from 0.5 to 1.5
- slot_mask: int32 [8, 8192], P(None, ('zc', 'zl')), may hold values 0 or 1
Outputs:
- new_velocity: float32 [8192, 3, 1536], P(('zc', 'zl'))
The draws below stay inside these ranges and needn't reach their ends.
All inputs are finite; a program needn't handle non-finite values. No bound on the sum of `slot_mask` on one device may be relied on, other than what follows from the above.
Results may differ from the reference program's by a relative error of at most 0.0003.
Values sent between devices are 32-bit elements; how exact they have to be, the bound alone decides.
No kernel may reach another device: no remote copies, remote signals or barrier semaphores. Data moves between devices by JAX's collectives and lax.ppermute only.
A program may use at most 64 MiB of HBM per device.

```python
import jax
import jax.numpy as jnp
from jax import lax

PLANES = 8
NY = 192
WALLROWS = 8
NZ = 8192


def draw_velocity(key, part):
    full_shape = (NZ, 3, PLANES * NY)
    return jnp.clip(jax.random.normal(key, full_shape, jnp.float32), -6.0, 6.0)


def with_ends(array, stream_key, least, top_value):
    dims = array.shape
    spot = [jax.random.randint(jax.random.fold_in(stream_key, axis), (), 0, dims[axis]) for axis in range(len(dims))]
    array = array.at[tuple(spot)].set(least)
    longest = dims.index(max(dims))
    spot[longest] = (spot[longest] + 1) % dims[longest]
    return array.at[tuple(spot)].set(top_value)


def setup_inputs(seed: int = 0) -> dict:
    keys = jax.random.split(jax.random.key(seed), 4)
    velocity = draw_velocity(jax.random.fold_in(keys[3], 71), 0)
    base_flow = jnp.clip(jax.random.uniform(keys[1], (NY,), jnp.float32, 0.5, 1.5), 0.5, 1.5)
    slot_mask = with_ends((jax.random.randint(keys[2], (WALLROWS, NZ), 0, 2) < 1).astype(jnp.int32), jax.random.fold_in(keys[2], 1), 0, 1)
    return {"velocity": velocity, "base_flow": base_flow, "slot_mask": slot_mask}


def explicit_part(field, normal_field, leading, base_flow, base_slope):
    ahead = jnp.roll(field, -1, axis=-2)
    behind = jnp.roll(field, 1, axis=-2)
    edge_zero = jnp.zeros_like(field[..., :1])
    upper = jnp.concatenate([field[..., 1:], edge_zero], axis=-1)
    lower = jnp.concatenate([edge_zero, field[..., :-1]], axis=-1)
    advect = -0.25 * base_flow * (ahead - behind)
    diffuse = 0.05 * (ahead + behind + upper + lower - 4.0 * field)
    return advect + diffuse - 0.25 * leading * base_slope * normal_field


def reference(velocity, base_flow, slot_mask):
    wall_rows = slot_mask.shape[0]
    shaped = velocity.reshape(NZ, 3, PLANES, NY)
    solid = (1 - slot_mask).astype(jnp.float32).T
    padded_base = jnp.pad(base_flow, 1)
    base_slope = padded_base[2:] - padded_base[:-2]
    wave_index = jnp.arange(NZ // 2 + 1)
    damping = jnp.where(wave_index <= NZ // 8, 1.0, 0.0).astype(jnp.float32)
    normal_field = shaped[:, 1]

    def one_component(component):
        field = lax.dynamic_index_in_dim(shaped, component, 1, keepdims=False)
        leading = (component == 0).astype(jnp.float32)
        forcing = explicit_part(field, normal_field, leading, base_flow, base_slope)
        near_wall = field[..., :wall_rows]
        plus_side = jnp.roll(near_wall, -1, axis=0)
        minus_side = jnp.roll(near_wall, 1, axis=0)
        wall_term = solid[:, None, :] * (0.15 * (plus_side + minus_side - 2.0 * near_wall) - 0.4 * near_wall)
        forcing = jnp.concatenate([forcing[..., :wall_rows] + wall_term, forcing[..., wall_rows:]], axis=-1)
        spectrum = jnp.fft.rfft(2.0 * field, axis=0)
        smoothed = jnp.fft.irfft(spectrum * damping[:, None, None], n=NZ, axis=0)
        return (smoothed - field) + forcing

    stacked = lax.map(one_component, jnp.arange(3))
    return jnp.moveaxis(stacked, 0, 1).reshape(NZ, 3, PLANES * NY)
```

```python
import functools
import math

import jax
import jax.numpy as jnp
import ml_dtypes
import numpy as np
from jax import lax
from jax.experimental import pallas as pl
from jax.experimental.pallas import tpu as pltpu
from jax.sharding import PartitionSpec as P

LANES = 128
AXES = ("zc", "zl")


def split_const(table):
    head = table.astype(ml_dtypes.bfloat16)
    tail = (table - head.astype(np.float64)).astype(ml_dtypes.bfloat16)
    return head, tail


@functools.cache
def tables(devices, span):
    length = devices * span
    half = devices // 2
    d = np.arange(devices)
    k = np.arange(half)
    turn = 2.0 * math.pi * (k[:, None] * d[None, :] % devices) / devices
    forward = np.concatenate([np.cos(turn), -np.sin(turn)], axis=0)
    forward[half] = 1.0 - 2.0 * (d % 2)
    weight = np.full(devices, 2.0)
    weight[0] = weight[half] = 1.0
    backward = forward.T * (2.0 * weight / devices)[None, :]
    j = np.arange(span)
    kept = length // 8
    count = 2 * kept // devices
    lag = j[:, None] - j[None, :]
    below = np.where(lag == 0, 1.0, span * np.sin(math.pi * lag / span))
    inner = np.where(lag == 0, count / span, np.sin(math.pi * count * lag / span) / below)
    inner_zero = np.where(lag == 0, (count + 1) / span, np.sin(math.pi * (count + 1) * lag / span) / below)
    twice = LANES // span
    inner = np.kron(np.eye(twice), inner)
    extra = np.kron(np.eye(twice), inner_zero) - inner
    angle = 2.0 * math.pi * (k - half)[:, None] * j[None, :] / length
    cos, sin = np.cos(angle), np.sin(angle)
    cos[0], sin[0] = 1.0, 0.0
    cos = np.tile(cos, (1, twice)).astype(np.float32)
    sin = np.tile(sin, (1, twice)).astype(np.float32)
    return (*split_const(forward), *split_const(inner), *split_const(extra), *split_const(backward), cos, sin)


def halves(values):
    head = values.astype(jnp.bfloat16)
    return head, (values - head.astype(jnp.float32)).astype(jnp.bfloat16)


def dot(a, b):
    return jnp.dot(a, b, preferred_element_type=jnp.float32)


def pack_kernel(v_ref, out_ref, first_ref, last_ref):
    comps, span, merged = v_ref.shape
    pairs = merged // (2 * LANES)
    for c in range(comps):
        for q in range(pairs):
            at = q * 2 * LANES
            both = jnp.concatenate([v_ref[c, :, at : at + LANES], v_ref[c, :, at + LANES : at + 2 * LANES]], axis=0)
            out_ref[pl.ds(c * pairs + q, LANES, stride=comps * pairs), :] = both.T
        first_ref[c : c + 1, :] = v_ref[c, 0:1, :]
        last_ref[c : c + 1, :] = v_ref[c, span - 1 : span, :]


def smooth_kernel(
    x_ref, fh_ref, fl_ref, rh_ref, rl_ref, eh_ref, el_ref, bh_ref, bl_ref, cos_ref, sin_ref, out_ref, z_ref, w_ref
):
    devices = fh_ref.shape[0]
    half = devices // 2
    groups = x_ref.shape[0] // devices
    cos, sin = cos_ref[...], sin_ref[...]
    fh, fl = fh_ref[...], fl_ref[...]
    rh, rl = rh_ref[...], rl_ref[...]
    bh, bl = bh_ref[...], bl_ref[...]
    zeros = []
    for p in range(groups):
        xh, xl = halves(x_ref[pl.ds(p, devices, stride=groups), :])
        y = dot(fh, xh) + dot(fh, xl) + dot(fl, xh)
        re, im = y[:half], y[half:]
        zeros.append(re[0:1])
        z_ref[p, :half] = re * cos + im * sin
        z_ref[p, half:] = im * cos - re * sin
    pad = -groups % 8
    zero_h, zero_l = halves(jnp.concatenate(zeros + [jnp.zeros((pad, LANES), jnp.float32)], axis=0))
    extra = dot(zero_h, eh_ref[...]) + dot(zero_l, eh_ref[...]) + dot(zero_h, el_ref[...])
    for p in range(groups):
        zh, zl = halves(z_ref[p])
        w = dot(zh, rh) + dot(zl, rh) + dot(zh, rl)
        re, im = w[:half], w[half:]
        w_ref[p, :half] = re * cos - im * sin
        w_ref[p, half:] = im * cos + re * sin
        w_ref[p, 0:1] = w_ref[p, 0:1] + extra[p : p + 1]
    for p in range(groups):
        wh, wl = halves(w_ref[p])
        out_ref[pl.ds(p, devices, stride=groups), :] = dot(bh, wh) + dot(bh, wl) + dot(bl, wh)


def forcing_kernel(v_ref, before_ref, after_ref, flow_ref, slope_ref, mask_ref, place_ref, out_ref, *, normal):
    comps, span, merged = v_ref.shape
    lane = lax.broadcasted_iota(jnp.int32, (1, merged), 1)
    row = lax.rem(lane, normal)
    not_top = (row < normal - 1).astype(jnp.float32)
    not_bottom = (row > 0).astype(jnp.float32)
    solid_rows = (1 - mask_ref[...]).astype(jnp.float32)
    solid = lax.dot_general(
        solid_rows.astype(jnp.bfloat16),
        place_ref[...],
        (((0,), (0,)), ((), ())),
        preferred_element_type=jnp.float32,
    )
    flow = -0.25 * flow_ref[...]
    slope = 0.25 * slope_ref[...]
    for c in range(comps):
        v = v_ref[c]
        ahead = pltpu.roll(v, merged - normal, 1)
        behind = pltpu.roll(v, normal, 1)
        upper = pltpu.roll(v, merged - 1, 1) * not_top
        lower = pltpu.roll(v, 1, 1) * not_bottom
        total = flow * (ahead - behind) + 0.05 * (ahead + behind + upper + lower - 4.0 * v)
        if c == 0:
            total = total - slope * v_ref[1]
        plus = jnp.concatenate([v[1:], after_ref[c : c + 1, :]], axis=0)
        minus = jnp.concatenate([before_ref[c : c + 1, :], v[:-1]], axis=0)
        total = total + solid * (0.15 * (plus + minus - 2.0 * v) - 0.4 * v)
        out_ref[c] = total - v


def unpack_kernel(s_ref, f_ref, out_ref):
    comps, span, merged = f_ref.shape
    pairs = merged // (2 * LANES)
    for c in range(comps):
        for q in range(pairs):
            both = s_ref[pl.ds(c * pairs + q, LANES, stride=comps * pairs), :].T
            lo = slice(q * 2 * LANES, q * 2 * LANES + LANES)
            hi = slice(q * 2 * LANES + LANES, (q + 1) * 2 * LANES)
            out_ref[c, :, lo] = f_ref[c, :, lo] + both[:span]
            out_ref[c, :, hi] = f_ref[c, :, hi] + both[span:]


def exchange(rows, devices):
    spread = lax.all_to_all(rows.reshape(devices, 1, -1), AXES, split_axis=0, concat_axis=0, tiled=True)
    return spread.reshape(rows.shape)


def body(velocity, base_flow, slot_mask):
    span, comps, merged = velocity.shape
    normal = base_flow.shape[0]
    planes = merged // normal
    wall_rows = slot_mask.shape[0]
    devices = lax.axis_size(AXES)
    groups = comps * merged // devices // (LANES // span)
    f32 = jnp.float32
    v = jnp.transpose(velocity, (1, 0, 2))
    edge = jax.ShapeDtypeStruct((comps, merged), f32)
    rows = jax.ShapeDtypeStruct((devices * groups, LANES), f32)
    sent, first, last = pl.pallas_call(pack_kernel, out_shape=(rows, edge, edge))(v)
    got = exchange(sent, devices)
    before = lax.ppermute(last, AXES, [(i, (i + 1) % devices) for i in range(devices)])
    after = lax.ppermute(first, AXES, [((i + 1) % devices, i) for i in range(devices)])
    padded = jnp.pad(base_flow, 1)
    flow = jnp.tile(base_flow, planes)[None]
    slope = jnp.tile(padded[2:] - padded[:-2], planes)[None]
    lane = np.arange(merged) % normal
    place = jnp.asarray((lane[None, :] == np.arange(wall_rows)[:, None]).astype(ml_dtypes.bfloat16))
    forcing = pl.pallas_call(
        functools.partial(forcing_kernel, normal=normal),
        out_shape=jax.ShapeDtypeStruct(v.shape, f32),
        cost_estimate=pl.CostEstimate(flops=30 * v.size, bytes_accessed=8 * v.size, transcendentals=0),
    )(v, before, after, flow, slope, slot_mask, place)
    smoothed = pl.pallas_call(
        smooth_kernel,
        out_shape=rows,
        scratch_shapes=[pltpu.VMEM((groups, devices, LANES), f32)] * 2,
    )(got, *(jnp.asarray(t) for t in tables(devices, span)))
    back = exchange(smoothed, devices)
    out = pl.pallas_call(unpack_kernel, out_shape=jax.ShapeDtypeStruct(v.shape, f32))(back, forcing)
    return jnp.transpose(out, (1, 0, 2))


def solution(mesh):
    in_specs = (P(AXES, None, None), P(), P(None, AXES))
    out_specs = P(AXES, None, None)
    return jax.shard_map(body, mesh=mesh, in_specs=in_specs, out_specs=out_specs, check_vma=False)
```

```python
import functools
import math

import jax
import jax.numpy as jnp
import ml_dtypes
import numpy as np
from jax import lax
from jax.experimental import pallas as pl
from jax.experimental.pallas import tpu as pltpu
from jax.sharding import PartitionSpec as P

LANES = 128
AXES = ("zc", "zl")


def split_const(table):
    head = table.astype(ml_dtypes.bfloat16)
    tail = (table - head.astype(np.float64)).astype(ml_dtypes.bfloat16)
    return head, tail


@functools.cache
def tables(devices, span):
    length = devices * span
    half = devices // 2
    d = np.arange(devices)
    k = np.arange(half)
    turn = 2.0 * math.pi * (k[:, None] * d[None, :] % devices) / devices
    forward = np.concatenate([np.cos(turn), -np.sin(turn)], axis=0)
    forward[half] = 1.0 - 2.0 * (d % 2)
    weight = np.full(devices, 2.0)
    weight[0] = weight[half] = 1.0
    backward = forward.T * (2.0 * weight / devices)[None, :]
    j = np.arange(span)
    kept = length // 8
    count = 2 * kept // devices
    lag = j[:, None] - j[None, :]
    below = np.where(lag == 0, 1.0, span * np.sin(math.pi * lag / span))
    inner = np.where(lag == 0, count / span, np.sin(math.pi * count * lag / span) / below)
    inner_zero = np.where(lag == 0, (count + 1) / span, np.sin(math.pi * (count + 1) * lag / span) / below)
    twice = LANES // span
    inner = np.kron(np.eye(twice), inner)
    extra = np.kron(np.eye(twice), inner_zero) - inner
    angle = 2.0 * math.pi * (k - half)[:, None] * j[None, :] / length
    cos, sin = np.cos(angle), np.sin(angle)
    cos[0], sin[0] = 1.0, 0.0
    cos = np.tile(cos, (1, twice)).astype(np.float32)
    sin = np.tile(sin, (1, twice)).astype(np.float32)
    return (both_rows(forward), both_lanes(inner), both_lanes(extra), both_rows(backward), cos, sin)


def both_rows(table):
    head, tail = split_const(table)
    return np.block([[head, head], [tail, tail]])


def both_lanes(table):
    head, tail = split_const(table)
    return np.block([[head, tail], [head, tail]])


def halves(values, axis):
    head = values.astype(jnp.bfloat16)
    tail = (values - head.astype(jnp.float32)).astype(jnp.bfloat16)
    return jnp.concatenate([head, tail], axis=axis)


def dot_rows(table, values):
    both = jnp.dot(table, halves(values, 0), preferred_element_type=jnp.float32)
    rows = table.shape[0] // 2
    return both[:rows] + both[rows:]


def dot_lanes(values, table):
    both = jnp.dot(halves(values, 1), table, preferred_element_type=jnp.float32)
    lanes = table.shape[1] // 2
    return both[:, :lanes] + both[:, lanes:]


def pack_kernel(v_ref, out_ref, first_ref, last_ref):
    _, span, merged = v_ref.shape
    c = pl.program_id(0)
    pairs = merged // (2 * LANES)
    groups = out_ref.shape[0] // LANES
    for q in range(pairs):
        at = q * 2 * LANES
        both = jnp.concatenate([v_ref[0, :, at : at + LANES], v_ref[0, :, at + LANES : at + 2 * LANES]], axis=0)
        out_ref[pl.ds(c * pairs + q, LANES, stride=groups), :] = both.T
    first_ref[pl.ds(c, 1), :] = v_ref[0, 0:1, :]
    last_ref[pl.ds(c, 1), :] = v_ref[0, span - 1 : span, :]


def smooth_kernel(x_ref, f_ref, r_ref, e_ref, b_ref, cos_ref, sin_ref, out_ref):
    devices = f_ref.shape[0] // 2
    half = devices // 2
    groups = x_ref.shape[0] // devices
    cos, sin = cos_ref[...], sin_ref[...]
    forward, inner, backward = f_ref[...], r_ref[...], b_ref[...]
    for p in range(0, groups, 2):
        pair = [x_ref[pl.ds(p + i, devices, stride=groups), :] for i in range(2)]
        y = dot_rows(forward, jnp.concatenate(pair, axis=1))
        turned = []
        for i in range(2):
            re = y[:half, i * LANES : (i + 1) * LANES]
            im = y[half:, i * LANES : (i + 1) * LANES]
            turned += [re * cos + im * sin, im * cos - re * sin]
        w = dot_lanes(jnp.concatenate(turned, axis=0), inner)
        lone = dot_lanes(jnp.concatenate([y[0:8, :LANES], y[0:8, LANES:]], axis=0), e_ref[...])
        back = []
        for i in range(2):
            re = w[i * devices : i * devices + half]
            im = w[i * devices + half : (i + 1) * devices]
            first = lax.broadcasted_iota(jnp.int32, (8, LANES), 0) == 0
            top = re * cos - im * sin
            top = jnp.concatenate([top[:8] + jnp.where(first, lone[i * 8 : (i + 1) * 8], 0.0), top[8:]], axis=0)
            back.append(jnp.concatenate([top, im * cos + re * sin], axis=0))
        y = dot_rows(backward, jnp.concatenate(back, axis=1))
        for i in range(2):
            out_ref[pl.ds(p + i, devices, stride=groups), :] = y[:, i * LANES : (i + 1) * LANES]


def forcing_kernel(v_ref, before_ref, after_ref, flow_ref, slope_ref, mask_ref, place_ref, out_ref, *, normal):
    comps, span, merged = v_ref.shape
    lane = lax.broadcasted_iota(jnp.int32, (1, merged), 1)
    row = lax.rem(lane, normal)
    not_top = (row < normal - 1).astype(jnp.float32)
    not_bottom = (row > 0).astype(jnp.float32)
    solid_rows = (1 - mask_ref[...]).astype(jnp.float32)
    solid = lax.dot_general(
        solid_rows.astype(jnp.bfloat16),
        place_ref[...],
        (((0,), (0,)), ((), ())),
        preferred_element_type=jnp.float32,
    )
    flow = -0.25 * flow_ref[...]
    slope = 0.25 * slope_ref[...]
    for c in range(comps):
        v = v_ref[c]
        ahead = pltpu.roll(v, merged - normal, 1)
        behind = pltpu.roll(v, normal, 1)
        upper = pltpu.roll(v, merged - 1, 1) * not_top
        lower = pltpu.roll(v, 1, 1) * not_bottom
        total = flow * (ahead - behind) + 0.05 * (ahead + behind + upper + lower - 4.0 * v)
        if c == 0:
            total = total - slope * v_ref[1]
        plus = jnp.concatenate([v[1:], after_ref[c : c + 1, :]], axis=0)
        minus = jnp.concatenate([before_ref[c : c + 1, :], v[:-1]], axis=0)
        total = total + solid * (0.15 * (plus + minus - 2.0 * v) - 0.4 * v)
        out_ref[c] = total - v


def unpack_kernel(s_ref, f_ref, out_ref):
    _, span, merged = out_ref.shape
    c = pl.program_id(0)
    pairs = merged // (2 * LANES)
    groups = s_ref.shape[0] // LANES
    for q in range(pairs):
        both = s_ref[pl.ds(c * pairs + q, LANES, stride=groups), :].T
        lo = slice(q * 2 * LANES, q * 2 * LANES + LANES)
        hi = slice(q * 2 * LANES + LANES, (q + 1) * 2 * LANES)
        out_ref[0, :, lo] = f_ref[c, :, lo] + both[:span]
        out_ref[0, :, hi] = f_ref[c, :, hi] + both[span:]


def exchange(rows, devices):
    spread = lax.all_to_all(rows.reshape(devices, 1, -1), AXES, split_axis=0, concat_axis=0, tiled=True)
    return spread.reshape(rows.shape)


def in_vmem(array):
    return pltpu.with_memory_space_constraint(array, pltpu.VMEM)


def body(velocity, base_flow, slot_mask):
    span, comps, merged = velocity.shape
    normal = base_flow.shape[0]
    planes = merged // normal
    wall_rows = slot_mask.shape[0]
    devices = lax.axis_size(AXES)
    groups = comps * merged // devices // (LANES // span)
    f32 = jnp.float32
    here = pl.BlockSpec(memory_space=pltpu.VMEM)
    part = pl.BlockSpec((1, span, merged), lambda c: (c, 0, 0))
    edge = pltpu.VMEM((comps, merged), f32)
    rows = pltpu.VMEM((devices * groups, LANES), f32)
    v = jnp.transpose(velocity, (1, 0, 2))
    sent, first, last = pl.pallas_call(
        pack_kernel, grid=(comps,), in_specs=[part], out_specs=(here,) * 3, out_shape=(rows, edge, edge)
    )(v)
    got = exchange(sent, devices)
    before = lax.ppermute(last, AXES, [(i, (i + 1) % devices) for i in range(devices)])
    after = lax.ppermute(first, AXES, [((i + 1) % devices, i) for i in range(devices)])
    got, before, after = lax.optimization_barrier((got, before, after))
    smoothed = pl.pallas_call(
        smooth_kernel,
        in_specs=[here] * 7,
        out_specs=here,
        out_shape=rows,
        cost_estimate=pl.CostEstimate(flops=0, bytes_accessed=10_000_000, transcendentals=0),
    )(in_vmem(got), *(in_vmem(jnp.asarray(t)) for t in tables(devices, span)))
    back = exchange(smoothed, devices)
    padded = jnp.pad(base_flow, 1)
    flow = jnp.tile(base_flow, planes)[None]
    slope = jnp.tile(padded[2:] - padded[:-2], planes)[None]
    lane = np.arange(merged) % normal
    place = jnp.asarray((lane[None, :] == np.arange(wall_rows)[:, None]).astype(ml_dtypes.bfloat16))
    forcing = pl.pallas_call(
        functools.partial(forcing_kernel, normal=normal),
        in_specs=[here] * 7,
        out_specs=here,
        out_shape=pltpu.VMEM(v.shape, f32),
        cost_estimate=pl.CostEstimate(flops=0, bytes_accessed=10_000_000, transcendentals=0),
    )(v, in_vmem(before), in_vmem(after), flow, slope, slot_mask, place)
    out = pl.pallas_call(
        unpack_kernel,
        grid=(comps,),
        in_specs=[here] * 2,
        out_specs=part,
        out_shape=jax.ShapeDtypeStruct(v.shape, f32),
    )(in_vmem(back), in_vmem(forcing))
    return jnp.transpose(out, (1, 0, 2))


def solution(mesh):
    in_specs = (P(AXES, None, None), P(), P(None, AXES))
    out_specs = P(AXES, None, None)
    return jax.shard_map(body, mesh=mesh, in_specs=in_specs, out_specs=out_specs, check_vma=False)
```

```python
import functools
import math

import jax
import jax.numpy as jnp
import ml_dtypes
import numpy as np
from jax import lax
from jax.experimental import pallas as pl
from jax.experimental.pallas import tpu as pltpu
from jax.sharding import PartitionSpec as P

LANES = 128
AXES = ("zc", "zl")


def split_const(table):
    head = table.astype(ml_dtypes.bfloat16)
    tail = (table - head.astype(np.float64)).astype(ml_dtypes.bfloat16)
    return head, tail


@functools.cache
def tables(devices, span):
    length = devices * span
    half = devices // 2
    d = np.arange(devices)
    k = np.arange(half)
    turn = 2.0 * math.pi * (k[:, None] * d[None, :] % devices) / devices
    forward = np.concatenate([np.cos(turn), -np.sin(turn)], axis=0)
    forward[half] = 1.0 - 2.0 * (d % 2)
    weight = np.full(devices, 2.0)
    weight[0] = weight[half] = 1.0
    backward = forward.T * (2.0 * weight / devices)[None, :]
    j = np.arange(span)
    kept = length // 8
    count = 2 * kept // devices
    lag = j[:, None] - j[None, :]
    below = np.where(lag == 0, 1.0, span * np.sin(math.pi * lag / span))
    inner = np.where(lag == 0, count / span, np.sin(math.pi * count * lag / span) / below)
    inner_zero = np.where(lag == 0, (count + 1) / span, np.sin(math.pi * (count + 1) * lag / span) / below)
    twice = LANES // span
    inner = np.kron(np.eye(twice), inner)
    extra = np.kron(np.eye(twice), inner_zero) - inner
    angle = 2.0 * math.pi * (k - half)[:, None] * j[None, :] / length
    cos, sin = np.cos(angle), np.sin(angle)
    cos[0], sin[0] = 1.0, 0.0
    cos = np.tile(cos, (1, twice)).astype(np.float32)
    sin = np.tile(sin, (1, twice)).astype(np.float32)
    return (both_rows(forward), both_lanes(inner), both_lanes(extra), both_rows(backward), cos, sin)


def both_rows(table):
    head, tail = split_const(table)
    return np.block([[head, head], [tail, tail]])


def both_lanes(table):
    head, tail = split_const(table)
    return np.block([[head, tail], [head, tail]])


def halves(values, axis):
    head = values.astype(jnp.bfloat16)
    tail = (values - head.astype(jnp.float32)).astype(jnp.bfloat16)
    return jnp.concatenate([head, tail], axis=axis)


def dot_rows(table, values):
    both = jnp.dot(table, halves(values, 0), preferred_element_type=jnp.float32)
    rows = table.shape[0] // 2
    return both[:rows] + both[rows:]


def dot_lanes(values, table):
    both = jnp.dot(halves(values, 1), table, preferred_element_type=jnp.float32)
    lanes = table.shape[1] // 2
    return both[:, :lanes] + both[:, lanes:]


def pack_kernel(v_ref, out_ref, first_ref, last_ref, held, sems):
    comps, span, merged = v_ref.shape
    pairs = merged // (2 * LANES)
    groups = out_ref.shape[0] // LANES
    steps = sems.shape[0]
    width = merged // steps
    loads = []
    for i in range(steps):
        piece = (slice(None), slice(None), pl.ds(i * width, width))
        loads.append(pltpu.make_async_copy(v_ref.at[piece], held.at[piece], sems.at[i]))
        loads[-1].start()
    for i in range(steps):
        loads[i].wait()
        for q in range(i * pairs // steps, (i + 1) * pairs // steps):
            at = q * 2 * LANES
            for c in range(comps):
                both = jnp.concatenate([held[c, :, at : at + LANES], held[c, :, at + LANES : at + 2 * LANES]], axis=0)
                out_ref[pl.ds(c * pairs + q, LANES, stride=groups), :] = both.T
    for c in range(comps):
        first_ref[c : c + 1, :] = held[c, 0:1, :]
        last_ref[c : c + 1, :] = held[c, span - 1 : span, :]


def smooth_kernel(x_ref, f_ref, r_ref, e_ref, b_ref, cos_ref, sin_ref, out_ref, z_ref, w_ref, lone_ref):
    devices = f_ref.shape[0] // 2
    half = devices // 2
    groups = x_ref.shape[0] // devices

    def outer(p):
        cos, sin = cos_ref[...], sin_ref[...]
        pair = [x_ref[pl.ds(p + i, devices, stride=groups), :] for i in range(2)]
        y = dot_rows(f_ref[...], jnp.concatenate(pair, axis=1))
        for i in range(2):
            at = (p + i) * devices
            re = y[:half, i * LANES : (i + 1) * LANES]
            im = y[half:, i * LANES : (i + 1) * LANES]
            z_ref[at : at + half, :] = re * cos + im * sin
            z_ref[at + half : at + devices, :] = im * cos - re * sin

    def inner(p):
        cos, sin = cos_ref[...], sin_ref[...]
        w = dot_lanes(z_ref[p * devices : (p + 2) * devices, :], r_ref[...])
        for i in range(2):
            at = (p + i) * LANES
            re = w[i * devices : i * devices + half]
            im = w[i * devices + half : (i + 1) * devices]
            w_ref[:half, at : at + LANES] = re * cos - im * sin
            w_ref[half:, at : at + LANES] = im * cos + re * sin

    def extra():
        rows = [z_ref[p * devices : p * devices + 1, :] for p in range(groups)]
        rows.append(jnp.zeros((-groups % 8, LANES), jnp.float32))
        lone = dot_lanes(jnp.concatenate(rows, axis=0), e_ref[...]) * (2.0 / devices)
        for p in range(groups):
            lone_ref[:, p * LANES : (p + 1) * LANES] = lone[p : p + 1]

    def outer_back(p):
        both = slice(p * LANES, (p + 2) * LANES)
        y = dot_rows(b_ref[...], w_ref[:, both]) + lone_ref[:, both]
        for i in range(2):
            out_ref[pl.ds(p + i, devices, stride=groups), :] = y[:, i * LANES : (i + 1) * LANES]

    for p in range(0, groups + 2, 2):
        if p < groups:
            outer(p)
        if p >= 2:
            inner(p - 2)
    extra()
    for p in range(0, groups, 2):
        outer_back(p)


def forcing_kernel(v_ref, flow_ref, slope_ref, mask_ref, place_ref, out_ref, gain_ref, *, normal):
    comps, span, merged = v_ref.shape
    lane = lax.broadcasted_iota(jnp.int32, (1, merged), 1)
    row = lax.rem(lane, normal)
    not_top = (row < normal - 1).astype(jnp.float32)
    not_bottom = (row > 0).astype(jnp.float32)
    solid_rows = (1 - mask_ref[...]).astype(jnp.float32)
    solid = lax.dot_general(
        solid_rows.astype(jnp.bfloat16),
        place_ref[...],
        (((0,), (0,)), ((), ())),
        preferred_element_type=jnp.float32,
    )
    flow = -0.25 * flow_ref[...]
    slope = 0.25 * slope_ref[...]
    nothing = jnp.zeros((1, merged), jnp.float32)
    gain_ref[0:1, :] = 0.15 * solid[0:1]
    gain_ref[1:2, :] = 0.15 * solid[span - 1 : span]
    for c in range(comps):
        v = v_ref[c]
        ahead = pltpu.roll(v, merged - normal, 1)
        behind = pltpu.roll(v, normal, 1)
        upper = pltpu.roll(v, merged - 1, 1) * not_top
        lower = pltpu.roll(v, 1, 1) * not_bottom
        total = flow * (ahead - behind) + 0.05 * (ahead + behind + upper + lower - 4.0 * v)
        if c == 0:
            total = total - slope * v_ref[1]
        plus = jnp.concatenate([v[1:], nothing], axis=0)
        minus = jnp.concatenate([nothing, v[:-1]], axis=0)
        total = total + solid * (0.15 * (plus + minus - 2.0 * v) - 0.4 * v)
        out_ref[c] = total - v


def unpack_kernel(s_ref, f_ref, gain_ref, before_ref, after_ref, out_ref, held, sems):
    comps, span, merged = f_ref.shape
    pairs = merged // (2 * LANES)
    groups = s_ref.shape[0] // LANES
    stores = []
    for c in range(comps):
        for q in range(pairs):
            both = s_ref[pl.ds(c * pairs + q, LANES, stride=groups), :].T
            lo = slice(q * 2 * LANES, q * 2 * LANES + LANES)
            hi = slice(q * 2 * LANES + LANES, (q + 1) * 2 * LANES)
            held[c, :, lo] = f_ref[c, :, lo] + both[:span]
            held[c, :, hi] = f_ref[c, :, hi] + both[span:]
        held[c, 0:1, :] = held[c, 0:1, :] + gain_ref[0:1, :] * before_ref[c : c + 1, :]
        held[c, span - 1 : span, :] = held[c, span - 1 : span, :] + gain_ref[1:2, :] * after_ref[c : c + 1, :]
        stores.append(pltpu.make_async_copy(held.at[c], out_ref.at[c], sems.at[c]))
        stores[-1].start()
    for store in stores:
        store.wait()


def exchange(rows, devices):
    spread = lax.all_to_all(rows.reshape(devices, 1, -1), AXES, split_axis=0, concat_axis=0, tiled=True)
    return spread.reshape(rows.shape)


def in_vmem(array):
    return pltpu.with_memory_space_constraint(array, pltpu.VMEM)


def body(velocity, base_flow, slot_mask):
    span, comps, merged = velocity.shape
    normal = base_flow.shape[0]
    planes = merged // normal
    wall_rows = slot_mask.shape[0]
    devices = lax.axis_size(AXES)
    groups = comps * merged // devices // (LANES // span)
    f32 = jnp.float32
    here = pl.BlockSpec(memory_space=pltpu.VMEM)
    away = pl.BlockSpec(memory_space=pltpu.HBM)
    edge = pltpu.VMEM((comps, merged), f32)
    rows = pltpu.VMEM((devices * groups, LANES), f32)
    v = jnp.transpose(velocity, (1, 0, 2))
    sent, first, last = pl.pallas_call(
        pack_kernel,
        in_specs=[away],
        out_specs=(here,) * 3,
        out_shape=(rows, edge, edge),
        scratch_shapes=[pltpu.VMEM(v.shape, f32), pltpu.SemaphoreType.DMA((3,))],
    )(v)
    got = exchange(sent, devices)
    smoothed = pl.pallas_call(
        smooth_kernel,
        in_specs=[here] * 7,
        out_specs=here,
        out_shape=rows,
        scratch_shapes=[
            pltpu.VMEM((groups * devices, LANES), f32),
            pltpu.VMEM((devices, groups * LANES), f32),
            pltpu.VMEM((1, groups * LANES), f32),
        ],
    )(in_vmem(got), *(in_vmem(jnp.asarray(t)) for t in tables(devices, span)))
    back = exchange(smoothed, devices)
    before = lax.ppermute(last, AXES, [(i, (i + 1) % devices) for i in range(devices)])
    after = lax.ppermute(first, AXES, [((i + 1) % devices, i) for i in range(devices)])
    padded = jnp.pad(base_flow, 1)
    flow = jnp.tile(base_flow, planes)[None]
    slope = jnp.tile(padded[2:] - padded[:-2], planes)[None]
    lane = np.arange(merged) % normal
    place = jnp.asarray((lane[None, :] == np.arange(wall_rows)[:, None]).astype(ml_dtypes.bfloat16))
    forcing, gain = pl.pallas_call(
        functools.partial(forcing_kernel, normal=normal),
        in_specs=[here] * 5,
        out_specs=(here,) * 2,
        out_shape=(pltpu.VMEM(v.shape, f32), pltpu.VMEM((2, merged), f32)),
        cost_estimate=pl.CostEstimate(flops=0, bytes_accessed=10_000_000, transcendentals=0),
    )(v, flow, slope, slot_mask, place)
    out = pl.pallas_call(
        unpack_kernel,
        in_specs=[here] * 5,
        out_specs=away,
        out_shape=jax.ShapeDtypeStruct(v.shape, f32),
        scratch_shapes=[pltpu.VMEM(v.shape, f32), pltpu.SemaphoreType.DMA((comps,))],
    )(in_vmem(back), in_vmem(forcing), in_vmem(gain), in_vmem(before), in_vmem(after))
    return jnp.transpose(out, (1, 0, 2))


def solution(mesh):
    in_specs = (P(AXES, None, None), P(), P(None, AXES))
    out_specs = P(AXES, None, None)
    return jax.shard_map(body, mesh=mesh, in_specs=in_specs, out_specs=out_specs, check_vma=False)
```

```python
import functools
import math

import jax
import jax.numpy as jnp
import ml_dtypes
import numpy as np
from jax import lax
from jax.experimental import pallas as pl
from jax.experimental.pallas import tpu as pltpu
from jax.sharding import PartitionSpec as P

LANES = 128
AXES = ("y", "z", "x", "core")
RANKS = ("core", "z", "x", "y")


def split_const(table):
    head = table.astype(ml_dtypes.bfloat16)
    tail = (table - head.astype(np.float64)).astype(ml_dtypes.bfloat16)
    return head, tail


@functools.cache
def tables(sizes, span):
    devices = math.prod(sizes)
    length = devices * span
    half = devices // 2
    d = np.arange(devices).reshape(sizes).transpose([AXES.index(a) for a in RANKS]).reshape(-1)
    k = np.arange(half)
    turn = 2.0 * math.pi * (k[:, None] * d[None, :] % devices) / devices
    forward = np.concatenate([np.cos(turn), -np.sin(turn)], axis=0)
    forward[half] = 1.0 - 2.0 * (d % 2)
    weight = np.full(devices, 2.0)
    weight[0] = weight[half] = 1.0
    backward = forward.T * (2.0 * weight / devices)[None, :]
    j = np.arange(span)
    kept = length // 8
    count = 2 * kept // devices
    lag = j[:, None] - j[None, :]
    below = np.where(lag == 0, 1.0, span * np.sin(math.pi * lag / span))
    inner = np.where(lag == 0, count / span, np.sin(math.pi * count * lag / span) / below)
    inner_zero = np.where(lag == 0, (count + 1) / span, np.sin(math.pi * (count + 1) * lag / span) / below)
    twice = LANES // span
    inner = np.kron(np.eye(twice), inner)
    extra = np.kron(np.eye(twice), inner_zero) - inner
    angle = 2.0 * math.pi * (k - half)[:, None] * j[None, :] / length
    cos, sin = np.cos(angle), np.sin(angle)
    cos[0], sin[0] = 1.0, 0.0
    cos = np.tile(cos, (1, twice)).astype(np.float32)
    sin = np.tile(sin, (1, twice)).astype(np.float32)
    return (both_rows(forward), both_lanes(inner), both_lanes(extra), both_rows(backward), cos, sin)


def both_rows(table):
    head, tail = split_const(table)
    return np.block([[head, head], [tail, tail]])


def both_lanes(table):
    head, tail = split_const(table)
    return np.block([[head, tail], [head, tail]])


def halves(values, axis):
    head = values.astype(jnp.bfloat16)
    tail = (values - head.astype(jnp.float32)).astype(jnp.bfloat16)
    return jnp.concatenate([head, tail], axis=axis)


def dot_rows(table, values):
    both = jnp.dot(table, halves(values, 0), preferred_element_type=jnp.float32)
    rows = table.shape[0] // 2
    return both[:rows] + both[rows:]


def dot_lanes(values, table):
    both = jnp.dot(halves(values, 1), table, preferred_element_type=jnp.float32)
    lanes = table.shape[1] // 2
    return both[:, :lanes] + both[:, lanes:]


def pack_kernel(v_ref, out_ref, first_ref, last_ref, held, sems):
    comps, span, merged = v_ref.shape
    pairs = merged // (2 * LANES)
    groups = out_ref.shape[0] // LANES
    steps = sems.shape[0]
    width = merged // steps
    loads = []
    for i in range(steps):
        piece = (slice(None), slice(None), pl.ds(i * width, width))
        loads.append(pltpu.make_async_copy(v_ref.at[piece], held.at[piece], sems.at[i]))
        loads[-1].start()
    for i in range(steps):
        loads[i].wait()
        for q in range(i * pairs // steps, (i + 1) * pairs // steps):
            at = q * 2 * LANES
            for c in range(comps):
                both = jnp.concatenate([held[c, :, at : at + LANES], held[c, :, at + LANES : at + 2 * LANES]], axis=0)
                out_ref[pl.ds(c * pairs + q, LANES, stride=groups), :] = both.T
    for c in range(comps):
        first_ref[c : c + 1, :] = held[c, 0:1, :]
        last_ref[c : c + 1, :] = held[c, span - 1 : span, :]


def smooth_kernel(x_ref, f_ref, r_ref, e_ref, b_ref, cos_ref, sin_ref, out_ref, z_ref, w_ref, lone_ref):
    devices = f_ref.shape[0] // 2
    half = devices // 2
    groups = x_ref.shape[0] // devices

    def outer(p):
        cos, sin = cos_ref[...], sin_ref[...]
        pair = [x_ref[pl.ds(p + i, devices, stride=groups), :] for i in range(2)]
        y = dot_rows(f_ref[...], jnp.concatenate(pair, axis=1))
        for i in range(2):
            at = (p + i) * devices
            re = y[:half, i * LANES : (i + 1) * LANES]
            im = y[half:, i * LANES : (i + 1) * LANES]
            z_ref[at : at + half, :] = re * cos + im * sin
            z_ref[at + half : at + devices, :] = im * cos - re * sin

    def inner(p):
        cos, sin = cos_ref[...], sin_ref[...]
        w = dot_lanes(z_ref[p * devices : (p + 2) * devices, :], r_ref[...])
        for i in range(2):
            at = (p + i) * LANES
            re = w[i * devices : i * devices + half]
            im = w[i * devices + half : (i + 1) * devices]
            w_ref[:half, at : at + LANES] = re * cos - im * sin
            w_ref[half:, at : at + LANES] = im * cos + re * sin

    def extra():
        rows = [z_ref[p * devices : p * devices + 1, :] for p in range(groups)]
        rows.append(jnp.zeros((-groups % 8, LANES), jnp.float32))
        lone = dot_lanes(jnp.concatenate(rows, axis=0), e_ref[...]) * (2.0 / devices)
        for p in range(groups):
            lone_ref[:, p * LANES : (p + 1) * LANES] = lone[p : p + 1]

    def outer_back(p):
        both = slice(p * LANES, (p + 2) * LANES)
        y = dot_rows(b_ref[...], w_ref[:, both]) + lone_ref[:, both]
        for i in range(2):
            out_ref[pl.ds(p + i, devices, stride=groups), :] = y[:, i * LANES : (i + 1) * LANES]

    for p in range(0, groups + 2, 2):
        if p < groups:
            outer(p)
        if p >= 2:
            inner(p - 2)
    extra()
    for p in range(0, groups, 2):
        outer_back(p)


def forcing_kernel(v_ref, flow_ref, slope_ref, mask_ref, place_ref, out_ref, gain_ref, *, normal):
    comps, span, merged = v_ref.shape
    lane = lax.broadcasted_iota(jnp.int32, (1, merged), 1)
    row = lax.rem(lane, normal)
    not_top = (row < normal - 1).astype(jnp.float32)
    not_bottom = (row > 0).astype(jnp.float32)
    solid_rows = (1 - mask_ref[...]).astype(jnp.float32)
    solid = lax.dot_general(
        solid_rows.astype(jnp.bfloat16),
        place_ref[...],
        (((0,), (0,)), ((), ())),
        preferred_element_type=jnp.float32,
    )
    flow = -0.25 * flow_ref[...]
    slope = 0.25 * slope_ref[...]
    nothing = jnp.zeros((1, merged), jnp.float32)
    gain_ref[0:1, :] = 0.15 * solid[0:1]
    gain_ref[1:2, :] = 0.15 * solid[span - 1 : span]
    for c in range(comps):
        v = v_ref[c]
        ahead = pltpu.roll(v, merged - normal, 1)
        behind = pltpu.roll(v, normal, 1)
        upper = pltpu.roll(v, merged - 1, 1) * not_top
        lower = pltpu.roll(v, 1, 1) * not_bottom
        total = flow * (ahead - behind) + 0.05 * (ahead + behind + upper + lower - 4.0 * v)
        if c == 0:
            total = total - slope * v_ref[1]
        plus = jnp.concatenate([v[1:], nothing], axis=0)
        minus = jnp.concatenate([nothing, v[:-1]], axis=0)
        total = total + solid * (0.15 * (plus + minus - 2.0 * v) - 0.4 * v)
        out_ref[c] = total - v


def unpack_kernel(s_ref, f_ref, gain_ref, before_ref, after_ref, out_ref, held, sems):
    comps, span, merged = f_ref.shape
    pairs = merged // (2 * LANES)
    groups = s_ref.shape[0] // LANES
    stores = []
    for c in range(comps):
        for q in range(pairs):
            both = s_ref[pl.ds(c * pairs + q, LANES, stride=groups), :].T
            lo = slice(q * 2 * LANES, q * 2 * LANES + LANES)
            hi = slice(q * 2 * LANES + LANES, (q + 1) * 2 * LANES)
            held[c, :, lo] = f_ref[c, :, lo] + both[:span]
            held[c, :, hi] = f_ref[c, :, hi] + both[span:]
        held[c, 0:1, :] = held[c, 0:1, :] + gain_ref[0:1, :] * before_ref[c : c + 1, :]
        held[c, span - 1 : span, :] = held[c, span - 1 : span, :] + gain_ref[1:2, :] * after_ref[c : c + 1, :]
        stores.append(pltpu.make_async_copy(held.at[c], out_ref.at[c], sems.at[c]))
        stores[-1].start()
    for store in stores:
        store.wait()


def exchange(rows, devices):
    spread = lax.all_to_all(rows.reshape(devices, 1, -1), RANKS, split_axis=0, concat_axis=0, tiled=True)
    return spread.reshape(rows.shape)


def in_vmem(array):
    return pltpu.with_memory_space_constraint(array, pltpu.VMEM)


def body(velocity, base_flow, slot_mask):
    span, comps, merged = velocity.shape
    normal = base_flow.shape[0]
    planes = merged // normal
    wall_rows = slot_mask.shape[0]
    sizes = tuple(lax.axis_size(a) for a in AXES)
    devices = math.prod(sizes)
    groups = comps * merged // devices // (LANES // span)
    f32 = jnp.float32
    here = pl.BlockSpec(memory_space=pltpu.VMEM)
    away = pl.BlockSpec(memory_space=pltpu.HBM)
    edge = pltpu.VMEM((comps, merged), f32)
    rows = pltpu.VMEM((devices * groups, LANES), f32)
    v = jnp.transpose(velocity, (1, 0, 2))
    sent, first, last = pl.pallas_call(
        pack_kernel,
        in_specs=[away],
        out_specs=(here,) * 3,
        out_shape=(rows, edge, edge),
        scratch_shapes=[pltpu.VMEM(v.shape, f32), pltpu.SemaphoreType.DMA((3,))],
    )(v)
    got = exchange(sent, devices)
    smoothed = pl.pallas_call(
        smooth_kernel,
        in_specs=[here] * 7,
        out_specs=here,
        out_shape=rows,
        scratch_shapes=[
            pltpu.VMEM((groups * devices, LANES), f32),
            pltpu.VMEM((devices, groups * LANES), f32),
            pltpu.VMEM((1, groups * LANES), f32),
        ],
    )(in_vmem(got), *(in_vmem(jnp.asarray(t)) for t in tables(sizes, span)))
    back = exchange(smoothed, devices)
    before = lax.ppermute(last, AXES, [(i, (i + 1) % devices) for i in range(devices)])
    after = lax.ppermute(first, AXES, [((i + 1) % devices, i) for i in range(devices)])
    padded = jnp.pad(base_flow, 1)
    flow = jnp.tile(base_flow, planes)[None]
    slope = jnp.tile(padded[2:] - padded[:-2], planes)[None]
    lane = np.arange(merged) % normal
    place = jnp.asarray((lane[None, :] == np.arange(wall_rows)[:, None]).astype(ml_dtypes.bfloat16))
    forcing, gain = pl.pallas_call(
        functools.partial(forcing_kernel, normal=normal),
        in_specs=[here] * 5,
        out_specs=(here,) * 2,
        out_shape=(pltpu.VMEM(v.shape, f32), pltpu.VMEM((2, merged), f32)),
        cost_estimate=pl.CostEstimate(flops=0, bytes_accessed=10_000_000, transcendentals=0),
    )(v, flow, slope, slot_mask, place)
    out = pl.pallas_call(
        unpack_kernel,
        in_specs=[here] * 5,
        out_specs=away,
        out_shape=jax.ShapeDtypeStruct(v.shape, f32),
        scratch_shapes=[pltpu.VMEM(v.shape, f32), pltpu.SemaphoreType.DMA((comps,))],
    )(in_vmem(back), in_vmem(forcing), in_vmem(gain), in_vmem(before), in_vmem(after))
    return jnp.transpose(out, (1, 0, 2))


def solution(mesh):
    outer, inner = mesh.devices.shape
    side = inner // 2
    torus = jax.sharding.Mesh(mesh.devices.reshape(outer // side, side, side, 2), AXES)
    in_specs = (P(AXES, None, None), P(), P(None, AXES))
    out_specs = P(AXES, None, None)
    return jax.shard_map(body, mesh=torus, in_specs=in_specs, out_specs=out_specs, check_vma=False)
```

```python
import functools
import math

import jax
import jax.numpy as jnp
import ml_dtypes
import numpy as np
from jax import lax
from jax.experimental import pallas as pl
from jax.experimental.pallas import tpu as pltpu
from jax.sharding import PartitionSpec as P

LANES = 128
AXES = ("y", "z", "x", "core")
RANKS = ("core", "z", "x", "y")
VMEM_LIMIT = 12 * 2**20


def split_const(table):
    head = table.astype(ml_dtypes.bfloat16)
    tail = (table - head.astype(np.float64)).astype(ml_dtypes.bfloat16)
    return head, tail


@functools.cache
def tables(sizes, span):
    devices = math.prod(sizes)
    length = devices * span
    half = devices // 2
    d = np.arange(devices).reshape(sizes).transpose([AXES.index(a) for a in RANKS]).reshape(-1)
    k = np.arange(half)
    turn = 2.0 * math.pi * (k[:, None] * d[None, :] % devices) / devices
    forward = np.concatenate([np.cos(turn), -np.sin(turn)], axis=0)
    forward[half] = 1.0 - 2.0 * (d % 2)
    weight = np.full(devices, 2.0)
    weight[0] = weight[half] = 1.0
    backward = forward.T * (2.0 * weight / devices)[None, :]
    j = np.arange(span)
    kept = length // 8
    count = 2 * kept // devices
    lag = j[:, None] - j[None, :]
    below = np.where(lag == 0, 1.0, span * np.sin(math.pi * lag / span))
    inner = np.where(lag == 0, count / span, np.sin(math.pi * count * lag / span) / below)
    inner_zero = np.where(lag == 0, (count + 1) / span, np.sin(math.pi * (count + 1) * lag / span) / below)
    twice = LANES // span
    inner = np.kron(np.eye(twice), inner)
    extra = np.kron(np.eye(twice), inner_zero) - inner
    angle = 2.0 * math.pi * (k - half)[:, None] * j[None, :] / length
    cos, sin = np.cos(angle), np.sin(angle)
    cos[0], sin[0] = 1.0, 0.0
    cos = np.tile(cos, (1, twice)).astype(np.float32)
    sin = np.tile(sin, (1, twice)).astype(np.float32)
    return (both_rows(forward), both_lanes(inner), both_lanes(extra), both_rows(backward), cos, sin)


def both_rows(table):
    head, tail = split_const(table)
    return np.block([[head, head], [tail, tail]])


def both_lanes(table):
    head, tail = split_const(table)
    return np.block([[head, tail], [head, tail]])


def halves(values, axis):
    head = values.astype(jnp.bfloat16)
    tail = (values - head.astype(jnp.float32)).astype(jnp.bfloat16)
    return jnp.concatenate([head, tail], axis=axis)


def dot_rows(table, values):
    both = jnp.dot(table, halves(values, 0), preferred_element_type=jnp.float32)
    rows = table.shape[0] // 2
    return both[:rows] + both[rows:]


def dot_lanes(values, table):
    both = jnp.dot(halves(values, 1), table, preferred_element_type=jnp.float32)
    lanes = table.shape[1] // 2
    return both[:, :lanes] + both[:, lanes:]


def pack_kernel(v_ref, out_ref, first_ref, last_ref, held, sems):
    comps, span, merged = v_ref.shape
    pairs = merged // (2 * LANES)
    groups = out_ref.shape[0] // LANES
    steps = sems.shape[0]
    width = merged // steps
    loads = []
    for i in range(steps):
        piece = (slice(None), slice(None), pl.ds(i * width, width))
        loads.append(pltpu.make_async_copy(v_ref.at[piece], held.at[piece], sems.at[i]))
        loads[-1].start()
    for i in range(steps):
        loads[i].wait()
        for q in range(i * pairs // steps, (i + 1) * pairs // steps):
            at = q * 2 * LANES
            for c in range(comps):
                both = jnp.concatenate([held[c, :, at : at + LANES], held[c, :, at + LANES : at + 2 * LANES]], axis=0)
                out_ref[pl.ds(c * pairs + q, LANES, stride=groups), :] = both.T
    for c in range(comps):
        first_ref[c : c + 1, :] = held[c, 0:1, :]
        last_ref[c : c + 1, :] = held[c, span - 1 : span, :]


def smooth_kernel(
    x_ref, f_ref, r_ref, e_ref, b_ref, cos_ref, sin_ref, _forcing, _gain, out_ref, z_ref, w_ref, lone_ref
):
    devices = f_ref.shape[0] // 2
    half = devices // 2
    groups = x_ref.shape[0] // devices

    def outer(p):
        cos, sin = cos_ref[...], sin_ref[...]
        pair = [x_ref[pl.ds(p + i, devices, stride=groups), :] for i in range(2)]
        y = dot_rows(f_ref[...], jnp.concatenate(pair, axis=1))
        for i in range(2):
            at = (p + i) * devices
            re = y[:half, i * LANES : (i + 1) * LANES]
            im = y[half:, i * LANES : (i + 1) * LANES]
            z_ref[at : at + half, :] = re * cos + im * sin
            z_ref[at + half : at + devices, :] = im * cos - re * sin

    def inner(p):
        cos, sin = cos_ref[...], sin_ref[...]
        w = dot_lanes(z_ref[p * devices : (p + 2) * devices, :], r_ref[...])
        for i in range(2):
            at = (p + i) * LANES
            re = w[i * devices : i * devices + half]
            im = w[i * devices + half : (i + 1) * devices]
            w_ref[:half, at : at + LANES] = re * cos - im * sin
            w_ref[half:, at : at + LANES] = im * cos + re * sin

    def extra():
        rows = [z_ref[p * devices : p * devices + 1, :] for p in range(groups)]
        rows.append(jnp.zeros((-groups % 8, LANES), jnp.float32))
        lone = dot_lanes(jnp.concatenate(rows, axis=0), e_ref[...]) * (2.0 / devices)
        for p in range(groups):
            lone_ref[:, p * LANES : (p + 1) * LANES] = lone[p : p + 1]

    def outer_back(p):
        both = slice(p * LANES, (p + 2) * LANES)
        y = dot_rows(b_ref[...], w_ref[:, both]) + lone_ref[:, both]
        for i in range(2):
            out_ref[pl.ds(p + i, devices, stride=groups), :] = y[:, i * LANES : (i + 1) * LANES]

    for p in range(0, groups + 2, 2):
        if p < groups:
            outer(p)
        if p >= 2:
            inner(p - 2)
    extra()
    for p in range(0, groups, 2):
        outer_back(p)


def forcing_kernel(v_ref, flow_ref, slope_ref, mask_ref, place_ref, out_ref, gain_ref, *, normal):
    comps, span, merged = v_ref.shape
    lane = lax.broadcasted_iota(jnp.int32, (1, merged), 1)
    row = lax.rem(lane, normal)
    not_top = (row < normal - 1).astype(jnp.float32)
    not_bottom = (row > 0).astype(jnp.float32)
    solid_rows = (1 - mask_ref[...]).astype(jnp.float32)
    solid = lax.dot_general(
        solid_rows.astype(jnp.bfloat16),
        place_ref[...],
        (((0,), (0,)), ((), ())),
        preferred_element_type=jnp.float32,
    )
    flow = -0.25 * flow_ref[...]
    slope = 0.25 * slope_ref[...]
    nothing = jnp.zeros((1, merged), jnp.float32)
    gain_ref[0:1, :] = 0.15 * solid[0:1]
    gain_ref[1:2, :] = 0.15 * solid[span - 1 : span]
    for c in range(comps):
        v = v_ref[c]
        ahead = pltpu.roll(v, merged - normal, 1)
        behind = pltpu.roll(v, normal, 1)
        upper = pltpu.roll(v, merged - 1, 1) * not_top
        lower = pltpu.roll(v, 1, 1) * not_bottom
        total = flow * (ahead - behind) + 0.05 * (ahead + behind + upper + lower - 4.0 * v)
        if c == 0:
            total = total - slope * v_ref[1]
        plus = jnp.concatenate([v[1:], nothing], axis=0)
        minus = jnp.concatenate([nothing, v[:-1]], axis=0)
        total = total + solid * (0.15 * (plus + minus - 2.0 * v) - 0.4 * v)
        out_ref[c] = total - v


def unpack_kernel(s_ref, f_ref, gain_ref, before_ref, after_ref, out_ref, held, sems):
    comps, span, merged = f_ref.shape
    pairs = merged // (2 * LANES)
    groups = s_ref.shape[0] // LANES
    stores = []
    for c in range(comps):
        for q in range(pairs):
            both = s_ref[pl.ds(c * pairs + q, LANES, stride=groups), :].T
            lo = slice(q * 2 * LANES, q * 2 * LANES + LANES)
            hi = slice(q * 2 * LANES + LANES, (q + 1) * 2 * LANES)
            held[c, :, lo] = f_ref[c, :, lo] + both[:span]
            held[c, :, hi] = f_ref[c, :, hi] + both[span:]
        held[c, 0:1, :] = held[c, 0:1, :] + gain_ref[0:1, :] * before_ref[c : c + 1, :]
        held[c, span - 1 : span, :] = held[c, span - 1 : span, :] + gain_ref[1:2, :] * after_ref[c : c + 1, :]
        stores.append(pltpu.make_async_copy(held.at[c], out_ref.at[c], sems.at[c]))
        stores[-1].start()
    for store in stores:
        store.wait()


def exchange(rows, devices):
    spread = lax.all_to_all(rows.reshape(devices, 1, -1), RANKS, split_axis=0, concat_axis=0, tiled=True)
    return spread.reshape(rows.shape)


def in_vmem(array):
    return pltpu.with_memory_space_constraint(array, pltpu.VMEM)


def body(velocity, base_flow, slot_mask):
    span, comps, merged = velocity.shape
    normal = base_flow.shape[0]
    planes = merged // normal
    wall_rows = slot_mask.shape[0]
    sizes = tuple(lax.axis_size(a) for a in AXES)
    devices = math.prod(sizes)
    groups = comps * merged // devices // (LANES // span)
    f32 = jnp.float32
    here = pl.BlockSpec(memory_space=pltpu.VMEM)
    away = pl.BlockSpec(memory_space=pltpu.HBM)
    edge = pltpu.VMEM((comps, merged), f32)
    rows = pltpu.VMEM((devices * groups, LANES), f32)
    v = pltpu.with_memory_space_constraint(jnp.transpose(velocity, (1, 0, 2)), pltpu.HBM)
    sent, first, last = pl.pallas_call(
        pack_kernel,
        compiler_params=pltpu.CompilerParams(vmem_limit_bytes=VMEM_LIMIT),
        in_specs=[away],
        out_specs=(here,) * 3,
        out_shape=(rows, edge, edge),
        scratch_shapes=[pltpu.VMEM(v.shape, f32), pltpu.SemaphoreType.DMA((3,))],
    )(v)
    got = exchange(sent, devices)
    before = lax.ppermute(last, AXES, [(i, (i + 1) % devices) for i in range(devices)])
    after = lax.ppermute(first, AXES, [((i + 1) % devices, i) for i in range(devices)])
    padded = jnp.pad(base_flow, 1)
    flow = jnp.tile(base_flow, planes)[None]
    slope = jnp.tile(padded[2:] - padded[:-2], planes)[None]
    lane = np.arange(merged) % normal
    place = jnp.asarray((lane[None, :] == np.arange(wall_rows)[:, None]).astype(ml_dtypes.bfloat16))
    forcing, gain = pl.pallas_call(
        functools.partial(forcing_kernel, normal=normal),
        compiler_params=pltpu.CompilerParams(vmem_limit_bytes=VMEM_LIMIT),
        in_specs=[here] * 5,
        out_specs=(here,) * 2,
        out_shape=(pltpu.VMEM(v.shape, f32), pltpu.VMEM((2, merged), f32)),
        cost_estimate=pl.CostEstimate(flops=0, bytes_accessed=10_000_000, transcendentals=0),
    )(v, flow, slope, slot_mask, place)
    smoothed = pl.pallas_call(
        smooth_kernel,
        compiler_params=pltpu.CompilerParams(vmem_limit_bytes=VMEM_LIMIT),
        in_specs=[here] * 9,
        out_specs=here,
        out_shape=rows,
        scratch_shapes=[
            pltpu.VMEM((groups * devices, LANES), f32),
            pltpu.VMEM((devices, groups * LANES), f32),
            pltpu.VMEM((1, groups * LANES), f32),
        ],
        cost_estimate=pl.CostEstimate(flops=0, bytes_accessed=1000, transcendentals=0),
    )(
        in_vmem(got),
        *(in_vmem(jnp.asarray(t)) for t in tables(sizes, span)),
        *(in_vmem(t) for t in (forcing, gain)),
    )
    smoothed, before, after = lax.optimization_barrier((smoothed, before, after))
    back = exchange(smoothed, devices)
    out = pl.pallas_call(
        unpack_kernel,
        compiler_params=pltpu.CompilerParams(vmem_limit_bytes=VMEM_LIMIT),
        in_specs=[here] * 5,
        out_specs=away,
        out_shape=jax.ShapeDtypeStruct(v.shape, f32),
        scratch_shapes=[pltpu.VMEM(v.shape, f32), pltpu.SemaphoreType.DMA((comps,))],
    )(in_vmem(back), in_vmem(forcing), in_vmem(gain), in_vmem(before), in_vmem(after))
    return jnp.transpose(out, (1, 0, 2))


def solution(mesh):
    outer, inner = mesh.devices.shape
    side = inner // 2
    torus = jax.sharding.Mesh(mesh.devices.reshape(outer // side, side, side, 2), AXES)
    in_specs = (P(AXES, None, None), P(), P(None, AXES))
    out_specs = P(AXES, None, None)
    return jax.shard_map(body, mesh=torus, in_specs=in_specs, out_specs=out_specs, check_vma=False)
```

```python
import functools
import math

import jax
import jax.numpy as jnp
import ml_dtypes
import numpy as np
from jax import lax
from jax.experimental import pallas as pl
from jax.experimental.pallas import tpu as pltpu
from jax.sharding import PartitionSpec as P

LANES = 128
AXES = ("y", "z", "x", "core")
RANKS = ("core", "z", "x", "y")
VMEM_LIMIT = 12 * 2**20


def split_const(table):
    head = table.astype(ml_dtypes.bfloat16)
    tail = (table - head.astype(np.float64)).astype(ml_dtypes.bfloat16)
    return head, tail


@functools.cache
def tables(sizes, span):
    devices = math.prod(sizes)
    length = devices * span
    half = devices // 2
    d = np.arange(devices).reshape(sizes).transpose([AXES.index(a) for a in RANKS]).reshape(-1)
    k = np.arange(half)
    turn = 2.0 * math.pi * (k[:, None] * d[None, :] % devices) / devices
    forward = np.concatenate([np.cos(turn), -np.sin(turn)], axis=0)
    forward[half] = 1.0 - 2.0 * (d % 2)
    weight = np.full(devices, 2.0)
    weight[0] = weight[half] = 1.0
    backward = forward.T * (2.0 * weight / devices)[None, :]
    j = np.arange(span)
    kept = length // 8
    count = 2 * kept // devices
    lag = j[:, None] - j[None, :]
    below = np.where(lag == 0, 1.0, span * np.sin(math.pi * lag / span))
    inner = np.where(lag == 0, count / span, np.sin(math.pi * count * lag / span) / below)
    inner_zero = np.where(lag == 0, (count + 1) / span, np.sin(math.pi * (count + 1) * lag / span) / below)
    twice = LANES // span
    inner = np.kron(np.eye(twice), inner)
    extra = np.kron(np.eye(twice), inner_zero) - inner
    angle = 2.0 * math.pi * (k - half)[:, None] * j[None, :] / length
    cos, sin = np.cos(angle), np.sin(angle)
    cos[0], sin[0] = 1.0, 0.0
    cos = np.tile(cos, (1, twice)).astype(np.float32)
    sin = np.tile(sin, (1, twice)).astype(np.float32)
    return (both_rows(forward), both_lanes(inner), both_lanes(extra), both_rows(backward), cos, sin)


def both_rows(table):
    head, tail = split_const(table)
    return np.block([[head, head], [tail, tail]])


def both_lanes(table):
    head, tail = split_const(table)
    return np.block([[head, tail], [head, tail]])


def halves(values, axis):
    head = values.astype(jnp.bfloat16)
    tail = (values - head.astype(jnp.float32)).astype(jnp.bfloat16)
    return jnp.concatenate([head, tail], axis=axis)


def dot_rows(table, values):
    both = jnp.dot(table, halves(values, 0), preferred_element_type=jnp.float32)
    rows = table.shape[0] // 2
    return both[:rows] + both[rows:]


def dot_lanes(values, table):
    both = jnp.dot(halves(values, 1), table, preferred_element_type=jnp.float32)
    lanes = table.shape[1] // 2
    return both[:, :lanes] + both[:, lanes:]


def pack_kernel(v_ref, out_ref, first_ref, last_ref, held, sems):
    comps, span, merged = v_ref.shape
    pairs = merged // (2 * LANES)
    groups = out_ref.shape[0] // LANES
    steps = sems.shape[0]
    width = merged // steps
    loads = []
    for i in range(steps):
        piece = (slice(None), slice(None), pl.ds(i * width, width))
        loads.append(pltpu.make_async_copy(v_ref.at[piece], held.at[piece], sems.at[i]))
        loads[-1].start()
    for i in range(steps):
        loads[i].wait()
        for q in range(i * pairs // steps, (i + 1) * pairs // steps):
            at = q * 2 * LANES
            for c in range(comps):
                both = jnp.concatenate([held[c, :, at : at + LANES], held[c, :, at + LANES : at + 2 * LANES]], axis=0)
                out_ref[pl.ds(c * pairs + q, LANES, stride=groups), :] = both.T
    for c in range(comps):
        first_ref[c : c + 1, :] = held[c, 0:1, :]
        last_ref[c : c + 1, :] = held[c, span - 1 : span, :]


def smooth_kernel(
    x_ref, f_ref, r_ref, e_ref, b_ref, cos_ref, sin_ref, _forcing, _gain, out_ref, z_ref, w_ref, lone_ref
):
    devices = f_ref.shape[0] // 2
    half = devices // 2
    groups = x_ref.shape[0] // devices

    block = math.gcd(groups, 6)

    def outer(p):
        cos, sin = cos_ref[...], sin_ref[...]
        lines = [x_ref[pl.ds(p + i, devices, stride=groups), :] for i in range(block)]
        y = dot_rows(f_ref[...], jnp.concatenate(lines, axis=1))
        for i in range(block):
            at = (p + i) * devices
            re = y[:half, i * LANES : (i + 1) * LANES]
            im = y[half:, i * LANES : (i + 1) * LANES]
            z_ref[at : at + half, :] = re * cos + im * sin
            z_ref[at + half : at + devices, :] = im * cos - re * sin

    def inner(p):
        cos, sin = cos_ref[...], sin_ref[...]
        w = dot_lanes(z_ref[p * devices : (p + block) * devices, :], r_ref[...])
        for i in range(block):
            at = (p + i) * LANES
            re = w[i * devices : i * devices + half]
            im = w[i * devices + half : (i + 1) * devices]
            w_ref[:half, at : at + LANES] = re * cos - im * sin
            w_ref[half:, at : at + LANES] = im * cos + re * sin

    def extra():
        rows = [z_ref[p * devices : p * devices + 1, :] for p in range(groups)]
        rows.append(jnp.zeros((-groups % 8, LANES), jnp.float32))
        lone = dot_lanes(jnp.concatenate(rows, axis=0), e_ref[...]) * (2.0 / devices)
        for p in range(groups):
            lone_ref[:, p * LANES : (p + 1) * LANES] = lone[p : p + 1]

    def outer_back(p):
        lines = slice(p * LANES, (p + block) * LANES)
        y = dot_rows(b_ref[...], w_ref[:, lines]) + lone_ref[:, lines]
        for i in range(block):
            out_ref[pl.ds(p + i, devices, stride=groups), :] = y[:, i * LANES : (i + 1) * LANES]

    for p in range(0, groups + block, block):
        if p < groups:
            outer(p)
        if p >= block:
            inner(p - block)
    extra()
    for p in range(0, groups, block):
        outer_back(p)


def forcing_kernel(v_ref, flow_ref, slope_ref, mask_ref, place_ref, out_ref, gain_ref, *, normal):
    comps, span, merged = v_ref.shape
    lane = lax.broadcasted_iota(jnp.int32, (1, merged), 1)
    row = lax.rem(lane, normal)
    not_top = (row < normal - 1).astype(jnp.float32)
    not_bottom = (row > 0).astype(jnp.float32)
    solid_rows = (1 - mask_ref[...]).astype(jnp.float32)
    solid = lax.dot_general(
        solid_rows.astype(jnp.bfloat16),
        place_ref[...],
        (((0,), (0,)), ((), ())),
        preferred_element_type=jnp.float32,
    )
    flow = -0.25 * flow_ref[...]
    slope = 0.25 * slope_ref[...]
    nothing = jnp.zeros((1, merged), jnp.float32)
    gain_ref[0:1, :] = 0.15 * solid[0:1]
    gain_ref[1:2, :] = 0.15 * solid[span - 1 : span]
    for c in range(comps):
        v = v_ref[c]
        ahead = pltpu.roll(v, merged - normal, 1)
        behind = pltpu.roll(v, normal, 1)
        upper = pltpu.roll(v, merged - 1, 1) * not_top
        lower = pltpu.roll(v, 1, 1) * not_bottom
        total = flow * (ahead - behind) + 0.05 * (ahead + behind + upper + lower - 4.0 * v)
        if c == 0:
            total = total - slope * v_ref[1]
        plus = jnp.concatenate([v[1:], nothing], axis=0)
        minus = jnp.concatenate([nothing, v[:-1]], axis=0)
        total = total + solid * (0.15 * (plus + minus - 2.0 * v) - 0.4 * v)
        out_ref[c] = total - v


def unpack_kernel(s_ref, f_ref, gain_ref, before_ref, after_ref, out_ref, held, sems):
    comps, span, merged = f_ref.shape
    pairs = merged // (2 * LANES)
    groups = s_ref.shape[0] // LANES
    parts = sems.shape[0] // comps
    width = merged // parts
    stores = []
    for c in range(comps):
        for h in range(parts):
            for q in range(h * pairs // parts, (h + 1) * pairs // parts):
                both = s_ref[pl.ds(c * pairs + q, LANES, stride=groups), :].T
                lo = slice(q * 2 * LANES, q * 2 * LANES + LANES)
                hi = slice(q * 2 * LANES + LANES, (q + 1) * 2 * LANES)
                held[c, :, lo] = f_ref[c, :, lo] + both[:span]
                held[c, :, hi] = f_ref[c, :, hi] + both[span:]
            part = slice(h * width, (h + 1) * width)
            low = gain_ref[0:1, part] * before_ref[c : c + 1, part]
            high = gain_ref[1:2, part] * after_ref[c : c + 1, part]
            held[c, 0:1, part] = held[c, 0:1, part] + low
            held[c, span - 1 : span, part] = held[c, span - 1 : span, part] + high
            piece = (c, slice(None), pl.ds(h * width, width))
            stores.append(pltpu.make_async_copy(held.at[piece], out_ref.at[piece], sems.at[c * parts + h]))
            stores[-1].start()
    for store in stores:
        store.wait()


def exchange(rows, devices):
    spread = lax.all_to_all(rows.reshape(devices, 1, -1), RANKS, split_axis=0, concat_axis=0, tiled=True)
    return spread.reshape(rows.shape)


def in_vmem(array):
    return pltpu.with_memory_space_constraint(array, pltpu.VMEM)


def body(velocity, base_flow, slot_mask):
    span, comps, merged = velocity.shape
    normal = base_flow.shape[0]
    planes = merged // normal
    wall_rows = slot_mask.shape[0]
    sizes = tuple(lax.axis_size(a) for a in AXES)
    devices = math.prod(sizes)
    groups = comps * merged // devices // (LANES // span)
    f32 = jnp.float32
    here = pl.BlockSpec(memory_space=pltpu.VMEM)
    away = pl.BlockSpec(memory_space=pltpu.HBM)
    edge = pltpu.VMEM((comps, merged), f32)
    rows = pltpu.VMEM((devices * groups, LANES), f32)
    v = pltpu.with_memory_space_constraint(jnp.transpose(velocity, (1, 0, 2)), pltpu.HBM)
    sent, first, last = pl.pallas_call(
        pack_kernel,
        compiler_params=pltpu.CompilerParams(vmem_limit_bytes=VMEM_LIMIT),
        in_specs=[away],
        out_specs=(here,) * 3,
        out_shape=(rows, edge, edge),
        scratch_shapes=[pltpu.VMEM(v.shape, f32), pltpu.SemaphoreType.DMA((3,))],
    )(v)
    got = exchange(sent, devices)
    before = lax.ppermute(last, AXES, [(i, (i + 1) % devices) for i in range(devices)])
    after = lax.ppermute(first, AXES, [((i + 1) % devices, i) for i in range(devices)])
    padded = jnp.pad(base_flow, 1)
    flow = jnp.tile(base_flow, planes)[None]
    slope = jnp.tile(padded[2:] - padded[:-2], planes)[None]
    lane = np.arange(merged) % normal
    place = jnp.asarray((lane[None, :] == np.arange(wall_rows)[:, None]).astype(ml_dtypes.bfloat16))
    forcing, gain = pl.pallas_call(
        functools.partial(forcing_kernel, normal=normal),
        compiler_params=pltpu.CompilerParams(vmem_limit_bytes=VMEM_LIMIT),
        in_specs=[here] * 5,
        out_specs=(here,) * 2,
        out_shape=(pltpu.VMEM(v.shape, f32), pltpu.VMEM((2, merged), f32)),
        cost_estimate=pl.CostEstimate(flops=0, bytes_accessed=10_000_000, transcendentals=0),
    )(v, flow, slope, slot_mask, place)
    smoothed = pl.pallas_call(
        smooth_kernel,
        compiler_params=pltpu.CompilerParams(vmem_limit_bytes=VMEM_LIMIT),
        in_specs=[here] * 9,
        out_specs=here,
        out_shape=rows,
        scratch_shapes=[
            pltpu.VMEM((groups * devices, LANES), f32),
            pltpu.VMEM((devices, groups * LANES), f32),
            pltpu.VMEM((1, groups * LANES), f32),
        ],
        cost_estimate=pl.CostEstimate(flops=0, bytes_accessed=1000, transcendentals=0),
    )(
        in_vmem(got),
        *(in_vmem(jnp.asarray(t)) for t in tables(sizes, span)),
        *(in_vmem(t) for t in (forcing, gain)),
    )
    smoothed, before, after = lax.optimization_barrier((smoothed, before, after))
    back = exchange(smoothed, devices)
    out = pl.pallas_call(
        unpack_kernel,
        compiler_params=pltpu.CompilerParams(vmem_limit_bytes=VMEM_LIMIT),
        in_specs=[here] * 5,
        out_specs=away,
        out_shape=jax.ShapeDtypeStruct(v.shape, f32),
        scratch_shapes=[pltpu.VMEM(v.shape, f32), pltpu.SemaphoreType.DMA((2 * comps,))],
    )(in_vmem(back), in_vmem(forcing), in_vmem(gain), in_vmem(before), in_vmem(after))
    return jnp.transpose(out, (1, 0, 2))


def solution(mesh):
    outer, inner = mesh.devices.shape
    side = inner // 2
    torus = jax.sharding.Mesh(mesh.devices.reshape(outer // side, side, side, 2), AXES)
    in_specs = (P(AXES, None, None), P(), P(None, AXES))
    out_specs = P(AXES, None, None)
    return jax.shard_map(body, mesh=torus, in_specs=in_specs, out_specs=out_specs, check_vma=False)
```

```python
import functools
import math

import jax
import jax.numpy as jnp
import ml_dtypes
import numpy as np
from jax import lax
from jax.experimental import pallas as pl
from jax.experimental.pallas import tpu as pltpu
from jax.sharding import PartitionSpec as P

LANES = 128
AXES = ("y", "z", "x", "core")
RANKS = ("core", "z", "x", "y")
VMEM_LIMIT = 12 * 2**20


def split_const(table):
    head = table.astype(ml_dtypes.bfloat16)
    tail = (table - head.astype(np.float64)).astype(ml_dtypes.bfloat16)
    return head, tail


@functools.cache
def tables(sizes, span):
    devices = math.prod(sizes)
    length = devices * span
    half = devices // 2
    d = np.arange(devices).reshape(sizes).transpose([AXES.index(a) for a in RANKS]).reshape(-1)
    k = np.arange(half)
    turn = 2.0 * math.pi * (k[:, None] * d[None, :] % devices) / devices
    forward = np.concatenate([np.cos(turn), -np.sin(turn)], axis=0)
    forward[half] = 1.0 - 2.0 * (d % 2)
    weight = np.full(devices, 2.0)
    weight[0] = weight[half] = 1.0
    backward = forward.T * (2.0 * weight / devices)[None, :]
    j = np.arange(span)
    kept = length // 8
    count = 2 * kept // devices
    lag = j[:, None] - j[None, :]
    below = np.where(lag == 0, 1.0, span * np.sin(math.pi * lag / span))
    inner = np.where(lag == 0, count / span, np.sin(math.pi * count * lag / span) / below)
    inner_zero = np.where(lag == 0, (count + 1) / span, np.sin(math.pi * (count + 1) * lag / span) / below)
    twice = LANES // span
    inner = np.kron(np.eye(twice), inner)
    extra = np.kron(np.eye(twice), inner_zero) - inner
    angle = 2.0 * math.pi * (k - half)[:, None] * j[None, :] / length
    cos, sin = np.cos(angle), np.sin(angle)
    cos[0], sin[0] = 1.0, 0.0
    cos = np.tile(cos, (1, twice)).astype(np.float32)
    sin = np.tile(sin, (1, twice)).astype(np.float32)
    return (both_rows(forward), both_lanes(inner), both_lanes(extra), both_rows(backward), cos, sin)


def both_rows(table):
    head, tail = split_const(table)
    return np.block([[head, head], [tail, tail]])


def both_lanes(table):
    head, tail = split_const(table)
    return np.block([[head, tail], [head, tail]])


def halves(values, axis):
    head = values.astype(jnp.bfloat16)
    tail = (values - head.astype(jnp.float32)).astype(jnp.bfloat16)
    return jnp.concatenate([head, tail], axis=axis)


def dot_rows(table, values):
    both = jnp.dot(table, halves(values, 0), preferred_element_type=jnp.float32)
    rows = table.shape[0] // 2
    return both[:rows] + both[rows:]


def dot_lanes(values, table):
    both = jnp.dot(halves(values, 1), table, preferred_element_type=jnp.float32)
    lanes = table.shape[1] // 2
    return both[:, :lanes] + both[:, lanes:]


def pack_kernel(v_ref, out_ref, first_ref, last_ref, held, turned, load_sems, store_sems):
    comps, span, merged = v_ref.shape
    pairs = merged // (2 * LANES)
    groups = out_ref.shape[0] // LANES
    steps = load_sems.shape[0]
    width = merged // steps
    loads = []
    for i in range(steps):
        piece = (slice(None), slice(None), pl.ds(i * width, width))
        loads.append(pltpu.make_async_copy(v_ref.at[piece], held.at[piece], load_sems.at[i]))
        loads[-1].start()
    stores = []
    by_device = (LANES, groups, LANES)
    for i in range(steps):
        loads[i].wait()
        low, high = i * pairs // steps, (i + 1) * pairs // steps
        for q in range(low, high):
            at = q * 2 * LANES
            for c in range(comps):
                both = jnp.concatenate([held[c, :, at : at + LANES], held[c, :, at + LANES : at + 2 * LANES]], axis=0)
                turned[pl.ds(q * comps + c, LANES, stride=groups), :] = both.T
        piece = (slice(None), pl.ds(low * comps, (high - low) * comps), slice(None))
        source, target = turned.reshape(by_device).at[piece], out_ref.reshape(by_device).at[piece]
        stores.append(pltpu.make_async_copy(source, target, store_sems.at[i]))
        stores[-1].start()
    for c in range(comps):
        first_ref[c : c + 1, :] = held[c, 0:1, :]
        last_ref[c : c + 1, :] = held[c, span - 1 : span, :]
    for store in stores:
        store.wait()


def smooth_kernel(
    x_ref, f_ref, r_ref, e_ref, b_ref, cos_ref, sin_ref, _forcing, _gain, out_ref, z_ref, w_ref, lone_ref
):
    devices = f_ref.shape[0] // 2
    half = devices // 2
    groups = x_ref.shape[0] // devices

    block = math.gcd(groups, 6)

    def outer(p):
        cos, sin = cos_ref[...], sin_ref[...]
        lines = [x_ref[pl.ds(p + i, devices, stride=groups), :] for i in range(block)]
        y = dot_rows(f_ref[...], jnp.concatenate(lines, axis=1))
        for i in range(block):
            at = (p + i) * devices
            re = y[:half, i * LANES : (i + 1) * LANES]
            im = y[half:, i * LANES : (i + 1) * LANES]
            z_ref[at : at + half, :] = re * cos + im * sin
            z_ref[at + half : at + devices, :] = im * cos - re * sin

    def inner(p):
        cos, sin = cos_ref[...], sin_ref[...]
        w = dot_lanes(z_ref[p * devices : (p + block) * devices, :], r_ref[...])
        for i in range(block):
            at = (p + i) * LANES
            re = w[i * devices : i * devices + half]
            im = w[i * devices + half : (i + 1) * devices]
            w_ref[:half, at : at + LANES] = re * cos - im * sin
            w_ref[half:, at : at + LANES] = im * cos + re * sin

    def extra():
        rows = [z_ref[p * devices : p * devices + 1, :] for p in range(groups)]
        rows.append(jnp.zeros((-groups % 8, LANES), jnp.float32))
        lone = dot_lanes(jnp.concatenate(rows, axis=0), e_ref[...]) * (2.0 / devices)
        for p in range(groups):
            lone_ref[:, p * LANES : (p + 1) * LANES] = lone[p : p + 1]

    def outer_back(p):
        lines = slice(p * LANES, (p + block) * LANES)
        y = dot_rows(b_ref[...], w_ref[:, lines]) + lone_ref[:, lines]
        for i in range(block):
            out_ref[pl.ds(p + i, devices, stride=groups), :] = y[:, i * LANES : (i + 1) * LANES]

    for p in range(0, groups + block, block):
        if p < groups:
            outer(p)
        if p >= block:
            inner(p - block)
    extra()
    for p in range(0, groups, block):
        outer_back(p)


def forcing_kernel(v_ref, flow_ref, slope_ref, mask_ref, place_ref, out_ref, gain_ref, *, normal):
    comps, span, merged = v_ref.shape
    lane = lax.broadcasted_iota(jnp.int32, (1, merged), 1)
    row = lax.rem(lane, normal)
    not_top = (row < normal - 1).astype(jnp.float32)
    not_bottom = (row > 0).astype(jnp.float32)
    solid_rows = (1 - mask_ref[...]).astype(jnp.float32)
    solid = lax.dot_general(
        solid_rows.astype(jnp.bfloat16),
        place_ref[...],
        (((0,), (0,)), ((), ())),
        preferred_element_type=jnp.float32,
    )
    flow = -0.25 * flow_ref[...]
    slope = 0.25 * slope_ref[...]
    nothing = jnp.zeros((1, merged), jnp.float32)
    gain_ref[0:1, :] = 0.15 * solid[0:1]
    gain_ref[1:2, :] = 0.15 * solid[span - 1 : span]
    for c in range(comps):
        v = v_ref[c]
        ahead = pltpu.roll(v, merged - normal, 1)
        behind = pltpu.roll(v, normal, 1)
        upper = pltpu.roll(v, merged - 1, 1) * not_top
        lower = pltpu.roll(v, 1, 1) * not_bottom
        total = flow * (ahead - behind) + 0.05 * (ahead + behind + upper + lower - 4.0 * v)
        if c == 0:
            total = total - slope * v_ref[1]
        plus = jnp.concatenate([v[1:], nothing], axis=0)
        minus = jnp.concatenate([nothing, v[:-1]], axis=0)
        total = total + solid * (0.15 * (plus + minus - 2.0 * v) - 0.4 * v)
        out_ref[c] = total - v


def unpack_kernel(s_ref, f_ref, gain_ref, before_ref, after_ref, out_ref, held, sems):
    comps, span, merged = f_ref.shape
    pairs = merged // (2 * LANES)
    groups = s_ref.shape[0] // LANES
    parts = sems.shape[0] // comps
    width = merged // parts
    stores = []
    for c in range(comps):
        for h in range(parts):
            for q in range(h * pairs // parts, (h + 1) * pairs // parts):
                both = s_ref[pl.ds(q * comps + c, LANES, stride=groups), :].T
                lo = slice(q * 2 * LANES, q * 2 * LANES + LANES)
                hi = slice(q * 2 * LANES + LANES, (q + 1) * 2 * LANES)
                held[c, :, lo] = f_ref[c, :, lo] + both[:span]
                held[c, :, hi] = f_ref[c, :, hi] + both[span:]
            part = slice(h * width, (h + 1) * width)
            low = gain_ref[0:1, part] * before_ref[c : c + 1, part]
            high = gain_ref[1:2, part] * after_ref[c : c + 1, part]
            held[c, 0:1, part] = held[c, 0:1, part] + low
            held[c, span - 1 : span, part] = held[c, span - 1 : span, part] + high
            piece = (c, slice(None), pl.ds(h * width, width))
            stores.append(pltpu.make_async_copy(held.at[piece], out_ref.at[piece], sems.at[c * parts + h]))
            stores[-1].start()
    for store in stores:
        store.wait()


def exchange(rows, devices):
    spread = lax.all_to_all(rows.reshape(devices, 1, -1), RANKS, split_axis=0, concat_axis=0, tiled=True)
    return spread.reshape(rows.shape)


def in_vmem(array):
    return pltpu.with_memory_space_constraint(array, pltpu.VMEM)


def body(velocity, base_flow, slot_mask):
    span, comps, merged = velocity.shape
    normal = base_flow.shape[0]
    planes = merged // normal
    wall_rows = slot_mask.shape[0]
    sizes = tuple(lax.axis_size(a) for a in AXES)
    devices = math.prod(sizes)
    groups = comps * merged // devices // (LANES // span)
    f32 = jnp.float32
    here = pl.BlockSpec(memory_space=pltpu.VMEM)
    away = pl.BlockSpec(memory_space=pltpu.HBM)
    edge = pltpu.VMEM((comps, merged), f32)
    rows = pltpu.VMEM((devices * groups, LANES), f32)
    v = pltpu.with_memory_space_constraint(jnp.transpose(velocity, (1, 0, 2)), pltpu.HBM)
    sent, first, last = pl.pallas_call(
        pack_kernel,
        compiler_params=pltpu.CompilerParams(vmem_limit_bytes=VMEM_LIMIT),
        in_specs=[away],
        out_specs=(away, here, here),
        out_shape=(pltpu.HBM(rows.shape, f32), edge, edge),
        scratch_shapes=[
            pltpu.VMEM(v.shape, f32),
            rows,
            pltpu.SemaphoreType.DMA((3,)),
            pltpu.SemaphoreType.DMA((3,)),
        ],
    )(v)
    got = exchange(sent, devices)
    before = lax.ppermute(last, AXES, [(i, (i + 1) % devices) for i in range(devices)])
    after = lax.ppermute(first, AXES, [((i + 1) % devices, i) for i in range(devices)])
    padded = jnp.pad(base_flow, 1)
    flow = jnp.tile(base_flow, planes)[None]
    slope = jnp.tile(padded[2:] - padded[:-2], planes)[None]
    lane = np.arange(merged) % normal
    place = jnp.asarray((lane[None, :] == np.arange(wall_rows)[:, None]).astype(ml_dtypes.bfloat16))
    forcing, gain = pl.pallas_call(
        functools.partial(forcing_kernel, normal=normal),
        compiler_params=pltpu.CompilerParams(vmem_limit_bytes=VMEM_LIMIT),
        in_specs=[here] * 5,
        out_specs=(here,) * 2,
        out_shape=(pltpu.VMEM(v.shape, f32), pltpu.VMEM((2, merged), f32)),
        cost_estimate=pl.CostEstimate(flops=0, bytes_accessed=10_000_000, transcendentals=0),
    )(v, flow, slope, slot_mask, place)
    smoothed = pl.pallas_call(
        smooth_kernel,
        compiler_params=pltpu.CompilerParams(vmem_limit_bytes=VMEM_LIMIT),
        in_specs=[here] * 9,
        out_specs=here,
        out_shape=rows,
        scratch_shapes=[
            pltpu.VMEM((groups * devices, LANES), f32),
            pltpu.VMEM((devices, groups * LANES), f32),
            pltpu.VMEM((1, groups * LANES), f32),
        ],
        cost_estimate=pl.CostEstimate(flops=0, bytes_accessed=1000, transcendentals=0),
    )(
        in_vmem(got),
        *(in_vmem(jnp.asarray(t)) for t in tables(sizes, span)),
        *(in_vmem(t) for t in (forcing, gain)),
    )
    smoothed, before, after = lax.optimization_barrier((smoothed, before, after))
    back = exchange(smoothed, devices)
    out = pl.pallas_call(
        unpack_kernel,
        compiler_params=pltpu.CompilerParams(vmem_limit_bytes=VMEM_LIMIT),
        in_specs=[here] * 5,
        out_specs=away,
        out_shape=jax.ShapeDtypeStruct(v.shape, f32),
        scratch_shapes=[pltpu.VMEM(v.shape, f32), pltpu.SemaphoreType.DMA((2 * comps,))],
    )(in_vmem(back), in_vmem(forcing), in_vmem(gain), in_vmem(before), in_vmem(after))
    return jnp.transpose(out, (1, 0, 2))


def solution(mesh):
    outer, inner = mesh.devices.shape
    side = inner // 2
    torus = jax.sharding.Mesh(mesh.devices.reshape(outer // side, side, side, 2), AXES)
    in_specs = (P(AXES, None, None), P(), P(None, AXES))
    out_specs = P(AXES, None, None)
    return jax.shard_map(body, mesh=torus, in_specs=in_specs, out_specs=out_specs, check_vma=False)
```

```python
import functools
import math

import jax
import jax.numpy as jnp
import ml_dtypes
import numpy as np
from jax import lax
from jax.experimental import pallas as pl
from jax.experimental.pallas import tpu as pltpu
from jax.sharding import PartitionSpec as P

LANES = 128
AXES = ("y", "z", "x", "core")
RANKS = ("core", "y", "x", "z")
VMEM_LIMIT = 12 * 2**20


def split_const(table):
    head = table.astype(ml_dtypes.bfloat16)
    tail = (table - head.astype(np.float64)).astype(ml_dtypes.bfloat16)
    return head, tail


@functools.cache
def tables(sizes, span):
    devices = math.prod(sizes)
    length = devices * span
    half = devices // 2
    d = np.arange(devices).reshape(sizes).transpose([AXES.index(a) for a in RANKS]).reshape(-1)
    k = np.arange(half)
    turn = 2.0 * math.pi * (k[:, None] * d[None, :] % devices) / devices
    forward = np.concatenate([np.cos(turn), -np.sin(turn)], axis=0)
    forward[half] = 1.0 - 2.0 * (d % 2)
    weight = np.full(devices, 2.0)
    weight[0] = weight[half] = 1.0
    backward = forward.T * (2.0 * weight / devices)[None, :]
    j = np.arange(span)
    kept = length // 8
    count = 2 * kept // devices
    lag = j[:, None] - j[None, :]
    below = np.where(lag == 0, 1.0, span * np.sin(math.pi * lag / span))
    inner = np.where(lag == 0, count / span, np.sin(math.pi * count * lag / span) / below)
    inner_zero = np.where(lag == 0, (count + 1) / span, np.sin(math.pi * (count + 1) * lag / span) / below)
    twice = LANES // span
    inner = np.kron(np.eye(twice), inner)
    extra = np.kron(np.eye(twice), inner_zero) - inner
    angle = 2.0 * math.pi * (k - half)[:, None] * j[None, :] / length
    cos, sin = np.cos(angle), np.sin(angle)
    cos[0], sin[0] = 1.0, 0.0
    cos = np.tile(cos, (1, twice)).astype(np.float32)
    sin = np.tile(sin, (1, twice)).astype(np.float32)
    return (both_rows(forward), both_lanes(inner), both_lanes(extra), both_rows(backward), cos, sin)


def both_rows(table):
    head, tail = split_const(table)
    return np.block([[head, head], [tail, tail]])


def both_lanes(table):
    head, tail = split_const(table)
    return np.block([[head, tail], [head, tail]])


def halves(values, axis):
    head = values.astype(jnp.bfloat16)
    tail = (values - head.astype(jnp.float32)).astype(jnp.bfloat16)
    return jnp.concatenate([head, tail], axis=axis)


def dot_rows(table, values):
    both = jnp.dot(table, halves(values, 0), preferred_element_type=jnp.float32)
    rows = table.shape[0] // 2
    return both[:rows] + both[rows:]


def dot_lanes(values, table):
    both = jnp.dot(halves(values, 1), table, preferred_element_type=jnp.float32)
    lanes = table.shape[1] // 2
    return both[:, :lanes] + both[:, lanes:]


def pack_kernel(v_ref, out_ref, first_ref, last_ref, held, turned, load_sems, store_sems):
    comps, span, merged = v_ref.shape
    pairs = merged // (2 * LANES)
    groups = out_ref.shape[0] // LANES
    steps = load_sems.shape[0]
    width = merged // steps
    loads = []
    for i in range(steps):
        piece = (slice(None), slice(None), pl.ds(i * width, width))
        loads.append(pltpu.make_async_copy(v_ref.at[piece], held.at[piece], load_sems.at[i]))
        loads[-1].start()
    stores = []
    by_device = (LANES, groups, LANES)
    for i in range(steps):
        loads[i].wait()
        low, high = i * pairs // steps, (i + 1) * pairs // steps
        for q in range(low, high):
            at = q * 2 * LANES
            for c in range(comps):
                both = jnp.concatenate([held[c, :, at : at + LANES], held[c, :, at + LANES : at + 2 * LANES]], axis=0)
                turned[pl.ds(q * comps + c, LANES, stride=groups), :] = both.T
        piece = (slice(None), pl.ds(low * comps, (high - low) * comps), slice(None))
        source, target = turned.reshape(by_device).at[piece], out_ref.reshape(by_device).at[piece]
        stores.append(pltpu.make_async_copy(source, target, store_sems.at[i]))
        stores[-1].start()
    for c in range(comps):
        first_ref[c : c + 1, :] = held[c, 0:1, :]
        last_ref[c : c + 1, :] = held[c, span - 1 : span, :]
    for store in stores:
        store.wait()


def smooth_kernel(
    x_ref, f_ref, r_ref, e_ref, b_ref, cos_ref, sin_ref, _forcing, _gain, out_ref, z_ref, w_ref, lone_ref
):
    devices = f_ref.shape[0] // 2
    half = devices // 2
    groups = x_ref.shape[0] // devices

    block = math.gcd(groups, 6)

    def outer(p):
        cos, sin = cos_ref[...], sin_ref[...]
        lines = [x_ref[pl.ds(p + i, devices, stride=groups), :] for i in range(block)]
        y = dot_rows(f_ref[...], jnp.concatenate(lines, axis=1))
        for i in range(block):
            at = (p + i) * devices
            re = y[:half, i * LANES : (i + 1) * LANES]
            im = y[half:, i * LANES : (i + 1) * LANES]
            z_ref[at : at + half, :] = re * cos + im * sin
            z_ref[at + half : at + devices, :] = im * cos - re * sin

    def inner(p):
        cos, sin = cos_ref[...], sin_ref[...]
        w = dot_lanes(z_ref[p * devices : (p + block) * devices, :], r_ref[...])
        for i in range(block):
            at = (p + i) * LANES
            re = w[i * devices : i * devices + half]
            im = w[i * devices + half : (i + 1) * devices]
            w_ref[:half, at : at + LANES] = re * cos - im * sin
            w_ref[half:, at : at + LANES] = im * cos + re * sin

    def extra():
        rows = [z_ref[p * devices : p * devices + 1, :] for p in range(groups)]
        rows.append(jnp.zeros((-groups % 8, LANES), jnp.float32))
        lone = dot_lanes(jnp.concatenate(rows, axis=0), e_ref[...]) * (2.0 / devices)
        for p in range(groups):
            lone_ref[:, p * LANES : (p + 1) * LANES] = lone[p : p + 1]

    def outer_back(p):
        lines = slice(p * LANES, (p + block) * LANES)
        y = dot_rows(b_ref[...], w_ref[:, lines]) + lone_ref[:, lines]
        for i in range(block):
            out_ref[pl.ds(p + i, devices, stride=groups), :] = y[:, i * LANES : (i + 1) * LANES]

    for p in range(0, groups + block, block):
        if p < groups:
            outer(p)
        if p >= block:
            inner(p - block)
    extra()
    for p in range(0, groups, block):
        outer_back(p)


def forcing_kernel(v_ref, flow_ref, slope_ref, mask_ref, place_ref, out_ref, gain_ref, *, normal):
    comps, span, merged = v_ref.shape
    lane = lax.broadcasted_iota(jnp.int32, (1, merged), 1)
    row = lax.rem(lane, normal)
    not_top = (row < normal - 1).astype(jnp.float32)
    not_bottom = (row > 0).astype(jnp.float32)
    solid_rows = (1 - mask_ref[...]).astype(jnp.float32)
    solid = lax.dot_general(
        solid_rows.astype(jnp.bfloat16),
        place_ref[...],
        (((0,), (0,)), ((), ())),
        preferred_element_type=jnp.float32,
    )
    flow = -0.25 * flow_ref[...]
    slope = 0.25 * slope_ref[...]
    nothing = jnp.zeros((1, merged), jnp.float32)
    gain_ref[0:1, :] = 0.15 * solid[0:1]
    gain_ref[1:2, :] = 0.15 * solid[span - 1 : span]
    for c in range(comps):
        v = v_ref[c]
        ahead = pltpu.roll(v, merged - normal, 1)
        behind = pltpu.roll(v, normal, 1)
        upper = pltpu.roll(v, merged - 1, 1) * not_top
        lower = pltpu.roll(v, 1, 1) * not_bottom
        total = flow * (ahead - behind) + 0.05 * (ahead + behind + upper + lower - 4.0 * v)
        if c == 0:
            total = total - slope * v_ref[1]
        plus = jnp.concatenate([v[1:], nothing], axis=0)
        minus = jnp.concatenate([nothing, v[:-1]], axis=0)
        total = total + solid * (0.15 * (plus + minus - 2.0 * v) - 0.4 * v)
        out_ref[c] = total - v


def unpack_kernel(s_ref, f_ref, gain_ref, before_ref, after_ref, out_ref, held, sems):
    comps, span, merged = f_ref.shape
    pairs = merged // (2 * LANES)
    groups = s_ref.shape[0] // LANES
    parts = sems.shape[0] // comps
    width = merged // parts
    stores = []
    for c in range(comps):
        for h in range(parts):
            for q in range(h * pairs // parts, (h + 1) * pairs // parts):
                both = s_ref[pl.ds(q * comps + c, LANES, stride=groups), :].T
                lo = slice(q * 2 * LANES, q * 2 * LANES + LANES)
                hi = slice(q * 2 * LANES + LANES, (q + 1) * 2 * LANES)
                held[c, :, lo] = f_ref[c, :, lo] + both[:span]
                held[c, :, hi] = f_ref[c, :, hi] + both[span:]
            part = slice(h * width, (h + 1) * width)
            low = gain_ref[0:1, part] * before_ref[c : c + 1, part]
            high = gain_ref[1:2, part] * after_ref[c : c + 1, part]
            held[c, 0:1, part] = held[c, 0:1, part] + low
            held[c, span - 1 : span, part] = held[c, span - 1 : span, part] + high
            piece = (c, slice(None), pl.ds(h * width, width))
            stores.append(pltpu.make_async_copy(held.at[piece], out_ref.at[piece], sems.at[c * parts + h]))
            stores[-1].start()
    for store in stores:
        store.wait()


def exchange(rows, devices):
    spread = lax.all_to_all(rows.reshape(devices, 1, -1), RANKS, split_axis=0, concat_axis=0, tiled=True)
    return spread.reshape(rows.shape)


def in_vmem(array):
    return pltpu.with_memory_space_constraint(array, pltpu.VMEM)


def body(velocity, base_flow, slot_mask):
    span, comps, merged = velocity.shape
    normal = base_flow.shape[0]
    planes = merged // normal
    wall_rows = slot_mask.shape[0]
    sizes = tuple(lax.axis_size(a) for a in AXES)
    devices = math.prod(sizes)
    groups = comps * merged // devices // (LANES // span)
    f32 = jnp.float32
    here = pl.BlockSpec(memory_space=pltpu.VMEM)
    away = pl.BlockSpec(memory_space=pltpu.HBM)
    edge = pltpu.VMEM((comps, merged), f32)
    rows = pltpu.VMEM((devices * groups, LANES), f32)
    v = pltpu.with_memory_space_constraint(jnp.transpose(velocity, (1, 0, 2)), pltpu.HBM)
    sent, first, last = pl.pallas_call(
        pack_kernel,
        compiler_params=pltpu.CompilerParams(vmem_limit_bytes=VMEM_LIMIT),
        in_specs=[away],
        out_specs=(away, here, here),
        out_shape=(pltpu.HBM(rows.shape, f32), edge, edge),
        scratch_shapes=[
            pltpu.VMEM(v.shape, f32),
            rows,
            pltpu.SemaphoreType.DMA((3,)),
            pltpu.SemaphoreType.DMA((3,)),
        ],
    )(v)
    got = exchange(sent, devices)
    before = lax.ppermute(last, AXES, [(i, (i + 1) % devices) for i in range(devices)])
    after = lax.ppermute(first, AXES, [((i + 1) % devices, i) for i in range(devices)])
    padded = jnp.pad(base_flow, 1)
    flow = jnp.tile(base_flow, planes)[None]
    slope = jnp.tile(padded[2:] - padded[:-2], planes)[None]
    lane = np.arange(merged) % normal
    place = jnp.asarray((lane[None, :] == np.arange(wall_rows)[:, None]).astype(ml_dtypes.bfloat16))
    forcing, gain = pl.pallas_call(
        functools.partial(forcing_kernel, normal=normal),
        compiler_params=pltpu.CompilerParams(vmem_limit_bytes=VMEM_LIMIT),
        in_specs=[here] * 5,
        out_specs=(here,) * 2,
        out_shape=(pltpu.VMEM(v.shape, f32), pltpu.VMEM((2, merged), f32)),
        cost_estimate=pl.CostEstimate(flops=0, bytes_accessed=10_000_000, transcendentals=0),
    )(v, flow, slope, slot_mask, place)
    smoothed = pl.pallas_call(
        smooth_kernel,
        compiler_params=pltpu.CompilerParams(vmem_limit_bytes=VMEM_LIMIT),
        in_specs=[here] * 9,
        out_specs=here,
        out_shape=rows,
        scratch_shapes=[
            pltpu.VMEM((groups * devices, LANES), f32),
            pltpu.VMEM((devices, groups * LANES), f32),
            pltpu.VMEM((1, groups * LANES), f32),
        ],
        cost_estimate=pl.CostEstimate(flops=0, bytes_accessed=1000, transcendentals=0),
    )(
        in_vmem(got),
        *(in_vmem(jnp.asarray(t)) for t in tables(sizes, span)),
        *(in_vmem(t) for t in (forcing, gain)),
    )
    smoothed, before, after = lax.optimization_barrier((smoothed, before, after))
    back = exchange(smoothed, devices)
    out = pl.pallas_call(
        unpack_kernel,
        compiler_params=pltpu.CompilerParams(vmem_limit_bytes=VMEM_LIMIT),
        in_specs=[here] * 5,
        out_specs=away,
        out_shape=jax.ShapeDtypeStruct(v.shape, f32),
        scratch_shapes=[pltpu.VMEM(v.shape, f32), pltpu.SemaphoreType.DMA((2 * comps,))],
    )(in_vmem(back), in_vmem(forcing), in_vmem(gain), in_vmem(before), in_vmem(after))
    return jnp.transpose(out, (1, 0, 2))


def solution(mesh):
    outer, inner = mesh.devices.shape
    side = inner // 2
    torus = jax.sharding.Mesh(mesh.devices.reshape(outer // side, side, side, 2), AXES)
    in_specs = (P(AXES, None, None), P(), P(None, AXES))
    out_specs = P(AXES, None, None)
    return jax.shard_map(body, mesh=torus, in_specs=in_specs, out_specs=out_specs, check_vma=False)
```
